512 devices in a mesh: seq: 8 (over x, core), dec: 64 (over y, z).
Axes of the slice: x: 4, y: 8, z: 8, core: 2. Of those that a mesh axis runs over, the one named last changes fastest.
Arguments:
- queries: bfloat16 [64, 1024, 32, 192], P('dec', 'seq'), may hold values from -96 to 96
- kv_latent: bfloat16 [64, 1024, 512], P('dec', 'seq'), may hold values from -6 to 6
- key_rope: bfloat16 [64, 1024, 64], P('dec', 'seq'), may hold values from -6 to 6
- kv_gain: bfloat16 [512], replicated, may hold values from 0.5 to 1.5
- w_kv_up: bfloat16 [512, 8192], P(None, 'seq'), may hold values from -0.25 to 0.25
- prefix_len: int32 [64], P('dec'), may hold values from 512 to 1024, as said below
- page_owner: int32 [64], replicated, may hold values from 0 to 63, as said below
- page_offset: int32 [64], replicated, may hold values from 0 to 8, as said below
Outputs:
- attn_out: bfloat16 [64, 1024, 4096], P('dec', 'seq')
- pool_latent: bfloat16 [64, 2048, 512], P('dec', 'seq')
- pool_rope: bfloat16 [64, 2048, 64], P('dec', 'seq')
The draws below stay inside these ranges and needn't reach their ends.
Inputs may be any that keep to these rules, and one draw needn't show every extreme that they name: `prefix_len`: some prefix has length 1024. `page_owner`: no owner receives more than 2 prefixes; some owner receives exactly 2. `page_offset`: A multiple of 8; prefixes with the same owner have distinct offsets.
All inputs are finite; a program needn't handle non-finite values.
Results may differ from the reference program's by a relative error of at most 0.011.
Values may be sent and summed in bfloat16 or wider, within the bound.
No kernel may reach another device: no remote copies, remote signals or barrier semaphores. Data moves between devices by JAX's collectives and lax.ppermute only.
A program may use at most 64 MiB of HBM per device.

```python
import jax
import jax.numpy as jnp
from jax import lax

HEADS = 32
NOPE = 128
ROPE = 64
VDIM = 128
LATENT = 512
PAGE = 16
MOST = 2
TOK_DEV = 128
SEQ_LEN = 1024
N_SEQ = 8
N_DEC = 64


def owner_blocks(key):
    first, second, third = jax.random.split(key, 3)
    total = N_DEC * MOST
    scores = jax.random.permutation(first, total).astype(jnp.int32)
    busiest = jax.random.randint(second, (), 0, N_DEC).astype(jnp.int32)
    owners = jnp.arange(total, dtype=jnp.int32) // MOST
    scores = scores + jnp.where(owners == busiest, total, 0).astype(jnp.int32)
    chosen = lax.top_k(scores, N_DEC)[1].astype(jnp.int32)
    chosen = jax.random.permutation(third, chosen).astype(jnp.int32)
    target_pos = ((busiest + N_DEC // 2) % N_DEC).astype(jnp.int32)
    where_first = jnp.argmax(chosen == busiest * MOST).astype(jnp.int32)
    at_target = chosen[target_pos]
    at_first = chosen[where_first]
    chosen = chosen.at[target_pos].set(at_first)
    chosen = chosen.at[where_first].set(at_target)
    return ((chosen // MOST).astype(jnp.int32), (chosen % MOST).astype(jnp.int32))


def draw_page_owner(key, part):
    return owner_blocks(key)[0]


def draw_page_offset(key, part):
    return owner_blocks(key)[1] * (TOK_DEV // PAGE)


def draw_prefix_len(key, part):
    key = jax.random.fold_in(key, 5)
    first, second = jax.random.split(key)
    full = TOK_DEV * N_SEQ
    lengths = jax.random.randint(first, (N_DEC,), full // 2, full + 1)
    longest = jax.random.randint(second, (), 0, N_DEC)
    return jnp.where(jnp.arange(N_DEC) == longest, full, lengths).astype(jnp.int32)


def draw_key_rope(key, part):
    key = jax.random.fold_in(key, 9)
    shape = (N_DEC, TOK_DEV * N_SEQ, ROPE)
    values = jnp.clip(jax.random.normal(key, shape, jnp.float32), -6.0, 6.0)
    return values.astype(jnp.bfloat16)


def draw_queries(key, part):
    key = jax.random.fold_in(key, 7)
    first = jax.random.fold_in(key, 0)
    shape = (N_DEC, TOK_DEV * N_SEQ, HEADS, NOPE + ROPE)
    values = jnp.clip(jax.random.normal(first, shape, jnp.float32), -6.0, 6.0)
    return values.astype(jnp.bfloat16)


def shard_levels(key, shape, pieces, least, top_value):
    factor_of = 1.0
    for position, blocks in pieces:
        steps = jax.random.uniform(jax.random.fold_in(jax.random.fold_in(key, 6), position), (blocks,), jnp.float32, least / len(pieces), top_value / len(pieces))
        factor_of = factor_of * jnp.repeat(jnp.exp(steps), shape[position] // blocks).reshape((-1,) + (1,) * (len(shape) - 1 - position))
    return factor_of


def noise(rng, dims, spread, bound, cuts=(), held_as=jnp.bfloat16):
    result = spread * jax.random.normal(rng, dims, jnp.float32)
    if cuts:
        result = result * shard_levels(rng, dims, cuts, -0.22, 0.18)
    return jnp.clip(result, -bound, bound).astype(held_as)


def setup_inputs(seed: int = 0) -> dict:
    arg_keys = jax.random.split(jax.random.key(seed), 9)
    return {
        "queries": draw_queries(jax.random.fold_in(arg_keys[8], 71), 0),
        "kv_latent": noise(arg_keys[1], (N_DEC, SEQ_LEN, LATENT), 1.0, 6.0, ((0, 64), (1, 8))),
        "key_rope": draw_key_rope(jax.random.fold_in(arg_keys[8], 71), 0),
        "kv_gain": jnp.clip(1.0 + 0.1 * jax.random.normal(arg_keys[3], (LATENT,), jnp.float32), 0.5, 1.5).astype(jnp.bfloat16),
        "w_kv_up": noise(arg_keys[4], (LATENT, HEADS * (NOPE + VDIM)), LATENT ** -0.5, 0.25, ((1, 8),)),
        "prefix_len": draw_prefix_len(jax.random.fold_in(arg_keys[8], 71), 0),
        "page_owner": draw_page_owner(jax.random.fold_in(arg_keys[8], 71), 0),
        "page_offset": draw_page_offset(jax.random.fold_in(arg_keys[8], 71), 0),
    }


def tables(positions, width):
    half = width // 2
    freq = jnp.exp(-jnp.log(50000.0) * jnp.arange(half, dtype=jnp.float32) * 2.0 / width)
    angle = positions.astype(jnp.float32)[:, None] * freq[None, :]
    return (jnp.cos(angle), jnp.sin(angle))

def rotate(values, cosine, sine):
    half = values.shape[-1] // 2
    first = values[..., :half]
    second = values[..., half:]
    return jnp.concatenate([first * cosine - second * sine, second * cosine + first * sine], axis=-1)

def normalize(latent, gain):
    values = latent.astype(jnp.float32)
    factor = lax.rsqrt(lax.optimization_barrier(jnp.mean(values * values, axis=-1, keepdims=True)) + 1e-06)
    return (values * factor * gain.astype(jnp.float32)).astype(jnp.bfloat16)

def reference(queries, kv_latent, key_rope, kv_gain, w_kv_up, prefix_len, page_owner, page_offset):
    length = queries.shape[1]
    heads = queries.shape[2]
    positions = jnp.arange(length, dtype=jnp.int32)
    cosine, sine = tables(positions, ROPE)
    latent = normalize(kv_latent, kv_gain)
    rope_keys = rotate(key_rope.astype(jnp.float32), cosine, sine).astype(jnp.bfloat16)
    factor = 1.0 / jnp.sqrt(jnp.float32(NOPE + ROPE))
    causal = positions[None, :] <= positions[:, None]

    def one_prefix(items):
        query, lat, rkeys, size = items
        kv = jnp.dot(lat, w_kv_up, preferred_element_type=jnp.float32).astype(jnp.bfloat16)
        kv = kv.reshape(length, heads, NOPE + VDIM)
        k_nope = kv[..., :NOPE]
        values = kv[..., NOPE:]
        q_rot = rotate(query[..., NOPE:].astype(jnp.float32), cosine[:, None, :], sine[:, None, :]).astype(jnp.bfloat16)
        q_full = jnp.concatenate([query[..., :NOPE], q_rot], axis=-1)
        k_full = jnp.concatenate([k_nope, jnp.broadcast_to(rkeys[:, None, :], (length, heads, ROPE))], axis=-1)
        scores = jnp.einsum('qhd,khd->hqk', q_full.astype(jnp.float32), k_full.astype(jnp.float32)) * factor
        masked = jnp.where(causal[None], scores, -jnp.inf)
        top = lax.optimization_barrier(jnp.max(masked, axis=-1, keepdims=True))
        probs = jnp.where(causal[None], jnp.exp(masked - top), 0.0)
        total = lax.optimization_barrier(jnp.sum(probs, axis=-1))
        weights = probs.astype(jnp.bfloat16)
        out = jnp.einsum('hqk,khd->qhd', weights.astype(jnp.float32), values.astype(jnp.float32))
        out = out / jnp.transpose(total)[:, :, None]
        out = jnp.where((positions < size)[:, None, None], out, 0.0)
        return out.astype(jnp.bfloat16).reshape(length, heads * VDIM)
    attn_out = lax.map(one_prefix, (queries, latent, rope_keys, prefix_len))
    seq_count = length // TOK_DEV
    pages_dev = TOK_DEV // PAGE
    kept = positions[None, :] < PAGE * ((prefix_len[:, None] + PAGE - 1) // PAGE)
    lat_kept = jnp.where(kept[:, :, None], latent, jnp.zeros_like(latent)).astype(jnp.float32)
    rope_kept = jnp.where(kept[:, :, None], rope_keys, jnp.zeros_like(rope_keys)).astype(jnp.float32)
    lat_kept = lat_kept.reshape(N_DEC, seq_count, TOK_DEV, LATENT)
    rope_kept = rope_kept.reshape(N_DEC, seq_count, TOK_DEV, ROPE)
    blocks = jnp.arange(MOST, dtype=jnp.int32)

    def one_owner(owner):
        select = ((page_owner[None, :] == owner) & (page_offset[None, :] == blocks[:, None] * pages_dev)).astype(jnp.float32)
        pool_l = jnp.einsum('bp,pstc->sbtc', select, lat_kept).reshape(seq_count * MOST * TOK_DEV, LATENT)
        pool_r = jnp.einsum('bp,pstc->sbtc', select, rope_kept).reshape(seq_count * MOST * TOK_DEV, ROPE)
        return (pool_l.astype(jnp.bfloat16), pool_r.astype(jnp.bfloat16))
    pool_latent, pool_rope = lax.map(one_owner, jnp.arange(N_DEC, dtype=jnp.int32))
    return (attn_out, pool_latent, pool_rope)
```

```python
import functools

import jax
import jax.numpy as jnp
import numpy as np
from jax import lax
from jax.experimental import pallas as pl
from jax.experimental.pallas import tpu as pltpu
from jax.sharding import PartitionSpec as P

NOPE = 128
ROPE = 64
HALF = ROPE // 2
QK = NOPE + ROPE
VDIM = 128
LATENT = 512
PAGE = 16
MOST = 2
WIDE = LATENT + 2 * ROPE
ROWS = 16
LANES = 128
FAR = -1e30
BF = jnp.bfloat16
F32 = jnp.float32
VMEM = pl.BlockSpec(memory_space=pltpu.VMEM)
SMEM = pl.BlockSpec(memory_space=pltpu.SMEM)


def rotation(length, toks):
    freq = 50000.0 ** (-2.0 * np.arange(HALF, dtype=np.float64) / ROPE)
    angle = freq[:, None] * np.arange(length, dtype=np.float64)[None, :]
    angle = angle.reshape(HALF, length // toks, toks).transpose(1, 0, 2)
    return np.cos(angle).astype(np.float32), np.sin(angle).astype(np.float32)


def prepare(seq_ref, len_ref, lat_ref, rope_ref, gain_ref, cos_ref, sin_ref, wide_ref, tiles_ref):
    toks = lat_ref.shape[0]
    x = lat_ref[...].astype(F32)
    scale = lax.rsqrt(jnp.mean(x * x, axis=-1, keepdims=True) + 1e-06)
    lat = x * scale * gain_ref[...][None, :].astype(F32)
    a = rope_ref[:HALF].astype(F32)
    b = rope_ref[HALF:].astype(F32)
    c = cos_ref[seq_ref[0]]
    s = sin_ref[seq_ref[0]]
    rot = jnp.concatenate([a * c - b * s, b * c + a * s], axis=0)
    wide_ref[:, :LATENT] = lat.astype(BF)
    padded = jnp.concatenate([rot, jnp.zeros_like(rot)], axis=0)
    wide_ref[:, LATENT:] = padded.T.astype(BF)
    kept = PAGE * ((len_ref[0] + PAGE - 1) // PAGE) - seq_ref[0] * toks
    rows = lax.broadcasted_iota(jnp.int32, lat.shape, 0)
    lat = jnp.where(rows < kept, lat, 0.0).astype(BF)
    lanes = lax.broadcasted_iota(jnp.int32, rot.shape, 1)
    rot = jnp.where(lanes < kept, rot, 0.0).astype(BF)
    across = LATENT // LANES
    down = toks // ROWS
    for i in range(down):
        for j in range(across):
            tiles_ref[i * across + j] = lat[
                ROWS * i : ROWS * (i + 1), LANES * j : LANES * (j + 1)
            ]
    for i in range(ROPE // ROWS):
        tiles_ref[down * across + i] = rot[ROWS * i : ROWS * (i + 1)]
    used = down * across + ROPE // ROWS
    tiles_ref[used:] = jnp.zeros_like(tiles_ref[used:])


def turn(owner_ref, offset_ref, got_ref, o_ref):
    o_ref[...] = jnp.zeros_like(o_ref)
    for p in range(got_ref.shape[0]):
        o_ref[owner_ref[p] * MOST + offset_ref[p] // 8] = got_ref[p]


def unpack(a_ref, lat_ref, rope_ref):
    toks = lat_ref.shape[0] // MOST
    across = LATENT // LANES
    down = toks // ROWS
    for m in range(MOST):
        for i in range(down):
            for j in range(across):
                lat_ref[
                    m * toks + ROWS * i : m * toks + ROWS * (i + 1), LANES * j : LANES * (j + 1)
                ] = a_ref[i * across + j, m]
        for i in range(ROPE // ROWS):
            rope_ref[ROWS * i : ROWS * (i + 1), m * toks : (m + 1) * toks] = a_ref[
                down * across + i, m
            ]


def attend(shifts, halves, seq_ref, len_ref, q_ref, p_ref, cos_ref, sin_ref, *rest):
    lat_refs, rest = rest[:4], rest[4:]
    count = len(shifts)
    w_refs = rest[: count * halves]
    own_ref, send_ref, lat_s, k_s, v_s, q_s, *w_s = rest[count * halves :]
    w_s = w_s[0] if w_s else None
    chips = len(lat_refs)
    toks = q_ref.shape[3]
    pair = 2 * toks
    s = seq_ref[0]
    c = s % 2
    x = s // 2
    size = len_ref[0]
    scale = float(np.log2(np.e) / np.sqrt(QK))
    row = lax.broadcasted_iota(jnp.int32, (pair, 1), 0)
    pos = jnp.where(row < toks, c * toks + row, (1 - c) * toks + row - toks)
    causal = lax.broadcasted_iota(jnp.int32, (pair, pair), 1) <= pos
    alive = x * pair + pos < size
    heads = own_ref.shape[2] // VDIM
    slots = k_s.shape[0]

    def queries(n, chip, i):
        base = i * QK
        for j, (ref, block) in enumerate(((q_ref, s), (p_ref, s + 1 - 2 * c))):
            span = slice(j * toks, (j + 1) * toks)
            a = ref[chip, c, base + NOPE : base + NOPE + HALF].astype(F32)
            b = ref[chip, c, base + NOPE + HALF : base + QK].astype(F32)
            co = cos_ref[block]
            si = sin_ref[block]
            rot = [a * co - b * si, b * co + a * si, ones]
            q_s[n, span, :NOPE] = ref[chip, c, base : base + NOPE].T
            q_s[n, span, NOPE:] = jnp.concatenate(rot, axis=0).astype(BF).T

    lane = lax.broadcasted_iota(jnp.int32, (pair, 2 * ROPE), 1)
    for k in range(chips):
        rows = slice(k * pair, (k + 1) * pair)
        lat_s[rows] = lat_refs[k][:, :LATENT]
        tail = lat_refs[k][:, LATENT:]
        if k:
            bias = jnp.where(k <= x, 0.0, FAR)
            tail = jnp.where(lane == ROPE, bias, tail.astype(F32)).astype(BF)
        for n in range(slots):
            k_s[n, rows, NOPE:] = tail
    ones = (lax.broadcasted_iota(jnp.int32, (ROPE, toks), 0) == 0).astype(F32)
    if halves > 1:
        depth = LATENT // halves
        for r in range(count * halves):
            w_s[r // halves, r % halves * depth : (r % halves + 1) * depth] = w_refs[r][...]
    w_all = w_refs if halves == 1 else [w_s.at[r] for r in range(count)]
    for r in range(count):
        chip = lax.rem(x + shifts[r], chips)
        for i in range(heads):
            n = (r * heads + i) % slots
            cols = slice(i * (NOPE + VDIM), (i + 1) * (NOPE + VDIM))
            kv = jnp.dot(
                lat_s[...], w_all[r][:, cols], preferred_element_type=F32
            )
            k_s[n, :, :NOPE] = kv[:, :NOPE].astype(BF)
            v_s[n] = kv[:, NOPE:].astype(BF)
            queries(n, chip, i)
            dots = lax.dot_general(
                q_s[n], k_s[n], (((1,), (1,)), ((), ())), preferred_element_type=F32
            )
            near = jnp.where(causal, dots[:, :pair], FAR)
            dots = jnp.concatenate([near, dots[:, pair:]], axis=1)
            top = jnp.max(dots, axis=1, keepdims=True)
            probs = jnp.exp2((dots - top) * scale)
            total = jnp.sum(probs, axis=1, keepdims=True)
            out = jnp.dot(probs.astype(BF), v_s[n], preferred_element_type=F32)
            out = jnp.where(alive, out / total, 0.0).astype(BF)
            own_ref[r, :, i * VDIM : (i + 1) * VDIM] = out[:toks]
            send_ref[r, :, i * VDIM : (i + 1) * VDIM] = out[toks:]


def lay_out(order, seq_ref, *refs):
    n = len(order)
    o_ref = refs[-1]
    chips = sum(len(shifts) for shifts in order)
    s = seq_ref[0]
    c = s % 2
    for g, shifts in enumerate(order):
        width = refs[g].shape[2]
        for r, shift in enumerate(shifts):
            base = lax.rem(s // 2 + shift, chips) * 2 * width
            mine = pl.multiple_of(base + c * width, width)
            other = pl.multiple_of(base + (1 - c) * width, width)
            o_ref[:, pl.ds(mine, width)] = refs[g][r]
            o_ref[:, pl.ds(other, width)] = refs[n + g][r]


def cost(flops, moved, exps=0):
    return pl.CostEstimate(flops=flops, bytes_accessed=moved, transcendentals=exps)


def shards(queries, kv_latent, key_rope, kv_gain, w_kv_up, prefix_len, page_owner, page_offset):
    toks = queries.shape[1]
    heads = queries.shape[2]
    n_seq = lax.axis_size("seq")
    n_dec = lax.axis_size("dec")
    chips = n_seq // 2
    length = toks * n_seq
    per = heads // n_seq
    cos, sin = rotation(length, toks)
    seq = jnp.reshape(lax.axis_index("seq"), (1,)).astype(jnp.int32)

    def along_x(a, k):
        return lax.ppermute(a, "seq", [(i, (i + 2 * k) % n_seq) for i in range(n_seq)])

    def partner(a):
        return lax.ppermute(a, "seq", [(i, i ^ 1) for i in range(n_seq)])

    w_left = along_x(w_kv_up, 1)
    w_right = along_x(w_kv_up, -1)
    depth = LATENT // 2
    w_far = (along_x(w_left[:depth], 1), along_x(w_right[depth:], -1))

    q = jnp.transpose(queries[0], (1, 2, 0)).reshape(chips, 2, per * QK, toks)
    q_partner = partner(q)

    wide, tiles = pl.pallas_call(
        prepare,
        in_specs=[SMEM, SMEM] + [VMEM] * 5,
        out_specs=[VMEM, VMEM],
        out_shape=[
            jax.ShapeDtypeStruct((toks, WIDE), BF),
            jax.ShapeDtypeStruct((n_dec, ROWS, LANES), BF),
        ],
        cost_estimate=cost(500000, 800000),
        name="prepare",
    )(seq, prefix_len, kv_latent[0], key_rope[0].T, kv_gain, cos, sin)

    pairs = [[2 * i, 2 * i + 1] for i in range(chips)]
    chip_wide = lax.all_gather(wide, "seq", axis=0, axis_index_groups=pairs, tiled=True)
    all_wide = [chip_wide] + [along_x(chip_wide, k) for k in range(1, chips)]

    got = lax.all_to_all(tiles, "dec", split_axis=0, concat_axis=0, tiled=True)
    turned = pl.pallas_call(
        turn,
        in_specs=[SMEM, SMEM, VMEM],
        out_specs=VMEM,
        out_shape=jax.ShapeDtypeStruct((n_dec * MOST, ROWS, LANES), BF),
        cost_estimate=cost(0, 800000),
        name="turn",
    )(page_owner, page_offset, got)
    pool = lax.all_to_all(
        turned.reshape(n_dec, MOST, ROWS, LANES), "dec", split_axis=0, concat_axis=0, tiled=True
    )

    order = ((0, chips - 1, 1), (2,))
    weights = ((w_kv_up, w_left, w_right), w_far)
    own, back = [], []
    for shifts, shard in zip(order, weights):
        n = len(shifts)
        a, b = pl.pallas_call(
            functools.partial(attend, shifts, len(shard) // n),
            in_specs=[SMEM, SMEM] + [VMEM] * (4 + chips + len(shard)),
            out_specs=[VMEM, VMEM],
            out_shape=[jax.ShapeDtypeStruct((n, toks, per * VDIM), BF)] * 2,
            scratch_shapes=[
                pltpu.VMEM((length, LATENT), BF),
                pltpu.VMEM((2, length, NOPE + 2 * ROPE), BF),
                pltpu.VMEM((2, length, VDIM), BF),
                pltpu.VMEM((2, 2 * toks, NOPE + 2 * ROPE), BF),
            ]
            + [pltpu.VMEM((n, LATENT, w_kv_up.shape[1]), BF)] * (len(shard) > n),
            compiler_params=pltpu.CompilerParams(vmem_limit_bytes=40 * 2**20),
            cost_estimate=cost(n * 2 * 10**9, n * 10**6, n * 10**6),
            name="attend",
        )(seq, prefix_len, q, q_partner, cos, sin, *all_wide, *shard)
        own.append(a)
        back.append(partner(b))

    attn_out = pl.pallas_call(
        functools.partial(lay_out, order),
        in_specs=[SMEM] + [VMEM] * (2 * len(order)),
        out_specs=VMEM,
        out_shape=jax.ShapeDtypeStruct((toks, heads * VDIM), BF),
        cost_estimate=cost(0, 2000000),
        name="lay_out",
    )(seq, *own, *back)

    pool_lat, pool_rope = pl.pallas_call(
        unpack,
        in_specs=[VMEM],
        out_specs=[VMEM, VMEM],
        out_shape=[
            jax.ShapeDtypeStruct((MOST * toks, LATENT), BF),
            jax.ShapeDtypeStruct((ROPE, MOST * toks), BF),
        ],
        cost_estimate=cost(0, 600000),
        name="unpack",
    )(pool)
    return attn_out[None], pool_lat[None], pool_rope.T[None]


def solution(mesh):
    return jax.shard_map(
        shards,
        mesh=mesh,
        in_specs=(
            P("dec", "seq", None, None),
            P("dec", "seq", None),
            P("dec", "seq", None),
            P(),
            P(None, "seq"),
            P("dec"),
            P(),
            P(),
        ),
        out_specs=(P("dec", "seq", None), P("dec", "seq", None), P("dec", "seq", None)),
        check_vma=False,
    )
```

```python
import functools

import jax
import jax.numpy as jnp
import numpy as np
from jax import lax
from jax.experimental import pallas as pl
from jax.experimental.pallas import tpu as pltpu
from jax.sharding import PartitionSpec as P

NOPE = 128
ROPE = 64
HALF = ROPE // 2
QK = NOPE + ROPE
VDIM = 128
LATENT = 512
PAGE = 16
MOST = 2
WIDE = LATENT + 2 * ROPE
ROWS = 16
LANES = 128
FAR = -1e30
BF = jnp.bfloat16
F32 = jnp.float32
VMEM = pl.BlockSpec(memory_space=pltpu.VMEM)
SMEM = pl.BlockSpec(memory_space=pltpu.SMEM)
ANY = pl.BlockSpec(memory_space=pl.ANY)


def rotation(length, toks):
    freq = 50000.0 ** (-2.0 * np.arange(HALF, dtype=np.float64) / ROPE)
    angle = freq[:, None] * np.arange(length, dtype=np.float64)[None, :]
    angle = angle.reshape(HALF, length // toks, toks).transpose(1, 0, 2)
    return np.cos(angle).astype(np.float32), np.sin(angle).astype(np.float32)


def prepare(seq_ref, len_ref, lat_ref, rope_ref, gain_ref, cos_ref, sin_ref, wide_ref, tiles_ref):
    toks = lat_ref.shape[0]
    x = lat_ref[...].astype(F32)
    scale = lax.rsqrt(jnp.mean(x * x, axis=-1, keepdims=True) + 1e-06)
    lat = x * scale * gain_ref[...][None, :].astype(F32)
    a = rope_ref[:HALF].astype(F32)
    b = rope_ref[HALF:].astype(F32)
    c = cos_ref[seq_ref[0]]
    s = sin_ref[seq_ref[0]]
    rot = jnp.concatenate([a * c - b * s, b * c + a * s], axis=0)
    wide_ref[:, :LATENT] = lat.astype(BF)
    padded = jnp.concatenate([rot, jnp.zeros_like(rot)], axis=0)
    wide_ref[:, LATENT:] = padded.T.astype(BF)
    kept = PAGE * ((len_ref[0] + PAGE - 1) // PAGE) - seq_ref[0] * toks
    rows = lax.broadcasted_iota(jnp.int32, lat.shape, 0)
    lat = jnp.where(rows < kept, lat, 0.0).astype(BF)
    lanes = lax.broadcasted_iota(jnp.int32, rot.shape, 1)
    rot = jnp.where(lanes < kept, rot, 0.0).astype(BF)
    across = LATENT // LANES
    down = toks // ROWS
    for i in range(down):
        for j in range(across):
            tiles_ref[i * across + j] = lat[
                ROWS * i : ROWS * (i + 1), LANES * j : LANES * (j + 1)
            ]
    for i in range(ROPE // ROWS):
        tiles_ref[down * across + i] = rot[ROWS * i : ROWS * (i + 1)]
    used = down * across + ROPE // ROWS
    tiles_ref[used:] = jnp.zeros_like(tiles_ref[used:])


def turn(dec_ref, owner_ref, offset_ref, got_ref, other_ref, o_ref):
    mine = dec_ref[0] % 2
    o_ref[...] = jnp.zeros_like(o_ref)
    for half, ref in ((mine, got_ref), (1 - mine, other_ref)):
        for i in range(ref.shape[0]):
            p = 2 * i + half
            owner = owner_ref[p]

            @pl.when(owner % 2 == mine)
            def _(ref=ref, i=i, p=p, owner=owner):
                o_ref[owner // 2 * MOST + offset_ref[p] // 8] = ref[i]


def attend(shifts, seq_ref, len_ref, q_ref, p_ref, cos_ref, sin_ref, *rest):
    chips = len(shifts)
    lat_refs, w_refs, rest = rest[:chips], rest[chips : 2 * chips + 1], rest[2 * chips + 1 :]
    own_ref, send_ref, raw_s, lat_s, tail_s, w_s, k_s, v_s, q_s, raw_sem, lat_sem, w_sem = rest
    toks = q_ref.shape[3]
    pair = 2 * toks
    s = seq_ref[0]
    c = s % 2
    x = s // 2

    lat_copies = []
    for k in range(chips):
        rows = pl.ds(k * pair, pair)
        lat_copies.append(
            pltpu.make_async_copy(
                lat_refs[k].at[:, pl.ds(0, LATENT)], lat_s.at[rows], lat_sem.at[0, k]
            )
        )
        lat_copies.append(
            pltpu.make_async_copy(
                lat_refs[k].at[:, pl.ds(LATENT, 2 * ROPE)], tail_s.at[rows], lat_sem.at[1, k]
            )
        )
    raw_copies = [
        pltpu.make_async_copy(ref.at[:, c], raw_s.at[j], raw_sem.at[j])
        for j, ref in enumerate((q_ref, p_ref))
    ]
    w_copies = [
        [pltpu.make_async_copy(w_refs[r], w_s.at[r], w_sem.at[r])] for r in range(chips - 1)
    ]
    depth = LATENT // 2
    w_copies.append(
        [
            pltpu.make_async_copy(
                w_refs[chips - 1 + j],
                w_s.at[chips - 1, pl.ds(j * depth, depth)],
                w_sem.at[chips - 1 + j],
            )
            for j in range(2)
        ]
    )
    for copy in lat_copies + w_copies[0] + raw_copies + sum(w_copies[1:], []):
        copy.start()

    size = len_ref[0]
    scale = float(np.log2(np.e) / np.sqrt(QK))
    row = lax.broadcasted_iota(jnp.int32, (pair, 1), 0)
    pos = jnp.where(row < toks, c * toks + row, (1 - c) * toks + row - toks)
    causal = lax.broadcasted_iota(jnp.int32, (pair, pair), 1) <= pos
    alive = x * pair + pos < size
    heads = own_ref.shape[2] // VDIM
    slots = k_s.shape[0]
    ones = (lax.broadcasted_iota(jnp.int32, (ROPE, toks), 0) == 0).astype(F32)

    def queries(n, chip, i):
        base = i * QK
        for j, block in enumerate((s, s + 1 - 2 * c)):
            span = slice(j * toks, (j + 1) * toks)
            a = raw_s[j, chip, base + NOPE : base + NOPE + HALF].astype(F32)
            b = raw_s[j, chip, base + NOPE + HALF : base + QK].astype(F32)
            co = cos_ref[block]
            si = sin_ref[block]
            rot = [a * co - b * si, b * co + a * si, ones]
            q_s[n, span, :NOPE] = raw_s[j, chip, base : base + NOPE].T
            q_s[n, span, NOPE:] = jnp.concatenate(rot, axis=0).astype(BF).T

    lane = lax.broadcasted_iota(jnp.int32, (pair, 2 * ROPE), 1)
    for copy in lat_copies:
        copy.wait()
    for k in range(chips):
        rows = slice(k * pair, (k + 1) * pair)
        tail = tail_s[rows]
        if k:
            bias = jnp.where(k <= x, 0.0, FAR)
            tail = jnp.where(lane == ROPE, bias, tail.astype(F32)).astype(BF)
        for n in range(slots):
            k_s[n, rows, NOPE:] = tail
    for r in range(chips):
        for copy in w_copies[r]:
            copy.wait()
        if r == 0:
            for copy in raw_copies:
                copy.wait()
        chip = lax.rem(x + shifts[r], chips)
        for i in range(heads):
            n = (r * heads + i) % slots
            cols = slice(i * (NOPE + VDIM), (i + 1) * (NOPE + VDIM))
            kv = jnp.dot(lat_s[...], w_s[r, :, cols], preferred_element_type=F32)
            k_s[n, :, :NOPE] = kv[:, :NOPE].astype(BF)
            v_s[n] = kv[:, NOPE:].astype(BF)
            queries(n, chip, i)
            dots = lax.dot_general(
                q_s[n], k_s[n], (((1,), (1,)), ((), ())), preferred_element_type=F32
            )
            near = jnp.where(causal, dots[:, :pair], FAR)
            dots = jnp.concatenate([near, dots[:, pair:]], axis=1)
            top = jnp.max(dots, axis=1, keepdims=True)
            probs = jnp.exp2((dots - top) * scale)
            total = jnp.sum(probs, axis=1, keepdims=True)
            out = jnp.dot(probs.astype(BF), v_s[n], preferred_element_type=F32)
            out = jnp.where(alive, out / total, 0.0).astype(BF)
            own_ref[r, :, i * VDIM : (i + 1) * VDIM] = out[:toks]
            send_ref[r, :, i * VDIM : (i + 1) * VDIM] = out[toks:]


def finish(shifts, seq_ref, own_ref, back_ref, pool_ref, o_ref, lat_ref, rope_ref):
    chips, _, width = own_ref.shape
    s = seq_ref[0]
    c = s % 2
    for r, shift in enumerate(shifts):
        base = lax.rem(s // 2 + shift, chips) * 2 * width
        mine = pl.multiple_of(base + c * width, width)
        other = pl.multiple_of(base + (1 - c) * width, width)
        o_ref[:, pl.ds(mine, width)] = own_ref[r]
        o_ref[:, pl.ds(other, width)] = back_ref[r]
    toks = lat_ref.shape[0] // MOST
    across = LATENT // LANES
    down = toks // ROWS
    for m in range(MOST):
        for i in range(down):
            for j in range(across):
                t = i * across + j
                lat_ref[
                    m * toks + ROWS * i : m * toks + ROWS * (i + 1), LANES * j : LANES * (j + 1)
                ] = pool_ref[t // 2, m, t % 2]
        for i in range(ROPE // ROWS):
            t = down * across + i
            rope_ref[ROWS * i : ROWS * (i + 1), m * toks : (m + 1) * toks] = pool_ref[
                t // 2, m, t % 2
            ]


def cost(flops, moved, exps=0):
    return pl.CostEstimate(flops=flops, bytes_accessed=moved, transcendentals=exps)


def shards(queries, kv_latent, key_rope, kv_gain, w_kv_up, prefix_len, page_owner, page_offset):
    toks = queries.shape[1]
    heads = queries.shape[2]
    n_seq = lax.axis_size("seq")
    n_dec = lax.axis_size("dec")
    chips = n_seq // 2
    length = toks * n_seq
    per = heads // n_seq
    cos, sin = rotation(length, toks)
    seq = jnp.reshape(lax.axis_index("seq"), (1,)).astype(jnp.int32)
    dec = jnp.reshape(lax.axis_index("dec"), (1,)).astype(jnp.int32)

    def along_x(a, k):
        return lax.ppermute(a, "seq", [(i, (i + 2 * k) % n_seq) for i in range(n_seq)])

    def partner(a):
        return lax.ppermute(a, "seq", [(i, i ^ 1) for i in range(n_seq)])

    w_left = along_x(w_kv_up, 1)
    w_right = along_x(w_kv_up, -1)
    depth = LATENT // 2
    w_far = (along_x(w_left[:depth], 1), along_x(w_right[depth:], -1))

    q = jnp.transpose(queries[0], (1, 2, 0)).reshape(chips, 2, per * QK, toks)
    q_partner = partner(q)

    wide, tiles = pl.pallas_call(
        prepare,
        in_specs=[SMEM, SMEM] + [VMEM] * 5,
        out_specs=[VMEM, VMEM],
        out_shape=[
            jax.ShapeDtypeStruct((toks, WIDE), BF),
            jax.ShapeDtypeStruct((n_dec, ROWS, LANES), BF),
        ],
        cost_estimate=cost(500000, 800000),
        name="prepare",
    )(seq, prefix_len, kv_latent[0], key_rope[0].T, kv_gain, cos, sin)

    pairs = [[2 * i, 2 * i + 1] for i in range(chips)]
    chip_wide = lax.all_gather(wide, "seq", axis=0, axis_index_groups=pairs, tiled=True)
    all_wide = [chip_wide] + [along_x(chip_wide, k) for k in range(1, chips)]

    halves = [list(range(h, n_dec, 2)) for h in range(2)]
    tiles = tiles.reshape(n_dec // 2, 2, ROWS, LANES)
    got = lax.all_to_all(tiles, "dec", 0, 0, axis_index_groups=halves, tiled=True)
    other = lax.ppermute(got, "dec", [(i, i ^ 1) for i in range(n_dec)])
    turned = pl.pallas_call(
        turn,
        in_specs=[SMEM, SMEM, SMEM, VMEM, VMEM],
        out_specs=VMEM,
        out_shape=jax.ShapeDtypeStruct((n_dec // 2 * MOST, 2, ROWS, LANES), BF),
        cost_estimate=cost(0, 800000),
        name="turn",
    )(dec, page_owner, page_offset, got, other)
    pool = lax.all_to_all(
        turned.reshape(n_dec // 2, MOST, 2, ROWS, LANES),
        "dec",
        0,
        0,
        axis_index_groups=halves,
        tiled=True,
    )

    shifts = (0, chips - 1, 1, 2)
    own, send = pl.pallas_call(
        functools.partial(attend, shifts),
        in_specs=[SMEM, SMEM, ANY, ANY, VMEM, VMEM] + [ANY] * (2 * chips + 1),
        out_specs=[VMEM, VMEM],
        out_shape=[jax.ShapeDtypeStruct((chips, toks, per * VDIM), BF)] * 2,
        scratch_shapes=[
            pltpu.VMEM((2, chips, per * QK, toks), BF),
            pltpu.VMEM((length, LATENT), BF),
            pltpu.VMEM((length, 2 * ROPE), BF),
            pltpu.VMEM((chips,) + w_kv_up.shape, BF),
            pltpu.VMEM((2, length, NOPE + 2 * ROPE), BF),
            pltpu.VMEM((2, length, VDIM), BF),
            pltpu.VMEM((2, 2 * toks, NOPE + 2 * ROPE), BF),
            pltpu.SemaphoreType.DMA((2,)),
            pltpu.SemaphoreType.DMA((2, chips)),
            pltpu.SemaphoreType.DMA((chips + 1,)),
        ],
        compiler_params=pltpu.CompilerParams(vmem_limit_bytes=32 * 2**20),
        cost_estimate=cost(8 * 10**9, 8 * 10**6, 4 * 10**6),
        name="attend",
    )(seq, prefix_len, q, q_partner, cos, sin, *all_wide, w_kv_up, w_left, w_right, *w_far)
    back = partner(send)

    used = (toks * (LATENT + ROPE)) // (2 * ROWS * LANES)
    attn_out, pool_lat, pool_rope = pl.pallas_call(
        functools.partial(finish, shifts),
        grid=(1,),
        in_specs=[
            SMEM,
            VMEM,
            VMEM,
            pl.BlockSpec((used, MOST, 2, ROWS, LANES), lambda i: (0, 0, 0, 0, 0)),
        ],
        out_specs=[VMEM, VMEM, VMEM],
        out_shape=[
            jax.ShapeDtypeStruct((toks, heads * VDIM), BF),
            jax.ShapeDtypeStruct((MOST * toks, LATENT), BF),
            jax.ShapeDtypeStruct((ROPE, MOST * toks), BF),
        ],
        cost_estimate=cost(0, 2500000),
        name="finish",
    )(seq, own, back, pool)
    return attn_out[None], pool_lat[None], pool_rope.T[None]


def solution(mesh):
    return jax.shard_map(
        shards,
        mesh=mesh,
        in_specs=(
            P("dec", "seq", None, None),
            P("dec", "seq", None),
            P("dec", "seq", None),
            P(),
            P(None, "seq"),
            P("dec"),
            P(),
            P(),
        ),
        out_specs=(P("dec", "seq", None), P("dec", "seq", None), P("dec", "seq", None)),
        check_vma=False,
    )
```

```python
import functools

import jax
import jax.numpy as jnp
import numpy as np
from jax import lax
from jax.experimental import pallas as pl
from jax.experimental.pallas import tpu as pltpu
from jax.sharding import PartitionSpec as P

NOPE = 128
ROPE = 64
HALF = ROPE // 2
QK = NOPE + ROPE
VDIM = 128
LATENT = 512
PAGE = 16
MOST = 2
WIDE = LATENT + 2 * ROPE
ROWS = 16
LANES = 128
FAR = -1e30
BF = jnp.bfloat16
F32 = jnp.float32
VMEM = pl.BlockSpec(memory_space=pltpu.VMEM)
SMEM = pl.BlockSpec(memory_space=pltpu.SMEM)
ANY = pl.BlockSpec(memory_space=pl.ANY)


def rotation(length, toks):
    freq = 50000.0 ** (-2.0 * np.arange(HALF, dtype=np.float64) / ROPE)
    angle = freq[:, None] * np.arange(length, dtype=np.float64)[None, :]
    angle = angle.reshape(HALF, length // toks, toks).transpose(1, 0, 2)
    return np.cos(angle).astype(np.float32), np.sin(angle).astype(np.float32)


def prepare(seq_ref, len_ref, lat_ref, rope_ref, gain_ref, cos_ref, sin_ref, wide_ref, tiles_ref):
    toks = lat_ref.shape[0]
    x = lat_ref[...].astype(F32)
    scale = lax.rsqrt(jnp.mean(x * x, axis=-1, keepdims=True) + 1e-06)
    lat = x * scale * gain_ref[...][None, :].astype(F32)
    a = rope_ref[:HALF].astype(F32)
    b = rope_ref[HALF:].astype(F32)
    c = cos_ref[seq_ref[0]]
    s = sin_ref[seq_ref[0]]
    rot = jnp.concatenate([a * c - b * s, b * c + a * s], axis=0)
    wide_ref[:, :LATENT] = lat.astype(BF)
    padded = jnp.concatenate([rot, jnp.zeros_like(rot)], axis=0)
    wide_ref[:, LATENT:] = padded.T.astype(BF)
    kept = PAGE * ((len_ref[0] + PAGE - 1) // PAGE) - seq_ref[0] * toks
    rows = lax.broadcasted_iota(jnp.int32, lat.shape, 0)
    lat = jnp.where(rows < kept, lat, 0.0).astype(BF)
    lanes = lax.broadcasted_iota(jnp.int32, rot.shape, 1)
    rot = jnp.where(lanes < kept, rot, 0.0).astype(BF)
    across = LATENT // LANES
    down = toks // ROWS
    for i in range(down):
        for j in range(across):
            tiles_ref[i * across + j] = lat[
                ROWS * i : ROWS * (i + 1), LANES * j : LANES * (j + 1)
            ]
    for i in range(ROPE // ROWS):
        tiles_ref[down * across + i] = rot[ROWS * i : ROWS * (i + 1)]
    used = down * across + ROPE // ROWS
    tiles_ref[used:] = jnp.zeros_like(tiles_ref[used:])


def turn(owner_ref, offset_ref, got_ref, o_ref):
    o_ref[...] = jnp.zeros_like(o_ref)
    for p in range(got_ref.shape[0]):
        o_ref[owner_ref[p] * MOST + offset_ref[p] // 8] = got_ref[p]


def attend(shifts, again, seq_ref, len_ref, q_ref, p_ref, cos_ref, sin_ref, *rest):
    count = len(shifts)
    chips = q_ref.shape[0]
    lat_refs, w_refs, rest = rest[:chips], rest[chips : chips + count], rest[chips + count :]
    rest = rest[2:] if again else rest
    out_ref, send_ref, raw_s, lat_s, tail_s, w_s, k_s, v_s, q_s, o_s, *sems = rest
    raw_sem, lat_sem, w_sem, out_sem = sems
    toks = q_ref.shape[3]
    pair = 2 * toks
    s = seq_ref[0]
    c = s % 2
    x = s // 2

    lat_copies = []
    for k in range(chips):
        rows = pl.ds(k * pair, pair)
        lat_copies.append(
            pltpu.make_async_copy(
                lat_refs[k].at[:, pl.ds(0, LATENT)], lat_s.at[rows], lat_sem.at[0, k]
            )
        )
        lat_copies.append(
            pltpu.make_async_copy(
                lat_refs[k].at[:, pl.ds(LATENT, 2 * ROPE)], tail_s.at[rows], lat_sem.at[1, k]
            )
        )
    raw_copies = [
        pltpu.make_async_copy(ref.at[:, c], raw_s.at[j], raw_sem.at[j])
        for j, ref in enumerate((q_ref, p_ref))
    ]
    w_copies = [
        pltpu.make_async_copy(w_refs[r], w_s.at[r], w_sem.at[r]) for r in range(count)
    ]
    for copy in lat_copies + w_copies[:1] + raw_copies + w_copies[1:]:
        copy.start()

    size = len_ref[0]
    scale = float(np.log2(np.e) / np.sqrt(QK))
    row = lax.broadcasted_iota(jnp.int32, (pair, 1), 0)
    pos = jnp.where(row < toks, c * toks + row, (1 - c) * toks + row - toks)
    causal = lax.broadcasted_iota(jnp.int32, (pair, pair), 1) <= pos
    alive = x * pair + pos < size
    width = o_s.shape[3]
    heads = width // VDIM
    out_copies = []
    slots = k_s.shape[0]
    ones = (lax.broadcasted_iota(jnp.int32, (ROPE, toks), 0) == 0).astype(F32)

    def queries(n, chip, i):
        base = i * QK
        for j, block in enumerate((s, s + 1 - 2 * c)):
            span = slice(j * toks, (j + 1) * toks)
            a = raw_s[j, chip, base + NOPE : base + NOPE + HALF].astype(F32)
            b = raw_s[j, chip, base + NOPE + HALF : base + QK].astype(F32)
            co = cos_ref[block]
            si = sin_ref[block]
            rot = [a * co - b * si, b * co + a * si, ones]
            q_s[n, span, :NOPE] = raw_s[j, chip, base : base + NOPE].T
            q_s[n, span, NOPE:] = jnp.concatenate(rot, axis=0).astype(BF).T

    lane = lax.broadcasted_iota(jnp.int32, (pair, 2 * ROPE), 1)
    for copy in lat_copies:
        copy.wait()
    for k in range(chips):
        rows = slice(k * pair, (k + 1) * pair)
        tail = tail_s[rows]
        if k:
            bias = jnp.where(k <= x, 0.0, FAR)
            tail = jnp.where(lane == ROPE, bias, tail.astype(F32)).astype(BF)
        for n in range(slots):
            k_s[n, rows, NOPE:] = tail
    for r in range(count):
        w_copies[r].wait()
        if r == 0:
            for copy in raw_copies:
                copy.wait()
        chip = lax.rem(x + shifts[r], chips)
        for i in range(heads):
            n = (r * heads + i) % slots
            cols = slice(i * (NOPE + VDIM), (i + 1) * (NOPE + VDIM))
            kv = jnp.dot(lat_s[...], w_s[r, :, cols], preferred_element_type=F32)
            k_s[n, :, :NOPE] = kv[:, :NOPE].astype(BF)
            v_s[n] = kv[:, NOPE:].astype(BF)
            queries(n, chip, i)
            dots = lax.dot_general(
                q_s[n], k_s[n], (((1,), (1,)), ((), ())), preferred_element_type=F32
            )
            near = jnp.where(causal, dots[:, :pair], FAR)
            dots = jnp.concatenate([near, dots[:, pair:]], axis=1)
            top = jnp.max(dots, axis=1, keepdims=True)
            probs = jnp.exp2((dots - top) * scale)
            total = jnp.sum(probs, axis=1, keepdims=True)
            out = jnp.dot(probs.astype(BF), v_s[n], preferred_element_type=F32)
            out = jnp.where(alive, out / total, 0.0).astype(BF)
            o_s[r, 0, :, i * VDIM : (i + 1) * VDIM] = out[:toks]
            o_s[r, 1, :, i * VDIM : (i + 1) * VDIM] = out[toks:]
        place = pl.ds(pl.multiple_of((2 * chip + c) * width, width), width)
        for j, to in enumerate((out_ref.at[:, place], send_ref.at[shifts[r]])):
            out_copies.append(pltpu.make_async_copy(o_s.at[r, j], to, out_sem.at[r, j]))
            out_copies[-1].start()
    for copy in out_copies:
        copy.wait()


def finish(seq_ref, back_ref, pool_ref, unused_ref, o_ref, lat_ref, rope_ref, sem):
    chips, _, width = back_ref.shape
    s = seq_ref[0]
    copies = []
    for r in range(chips):
        block = 2 * lax.rem(s // 2 + r, chips) + 1 - s % 2
        place = pl.ds(pl.multiple_of(block * width, width), width)
        copies.append(pltpu.make_async_copy(back_ref.at[r], o_ref.at[:, place], sem.at[r]))
        copies[-1].start()
    toks = lat_ref.shape[0] // MOST
    across = LATENT // LANES
    down = toks // ROWS
    for m in range(MOST):
        for i in range(down):
            for j in range(across):
                t = i * across + j
                lat_ref[
                    m * toks + ROWS * i : m * toks + ROWS * (i + 1), LANES * j : LANES * (j + 1)
                ] = pool_ref[t, m]
        for i in range(ROPE // ROWS):
            t = down * across + i
            rope_ref[ROWS * i : ROWS * (i + 1), m * toks : (m + 1) * toks] = pool_ref[t, m]
    for copy in copies:
        copy.wait()


def cost(flops, moved, exps=0):
    return pl.CostEstimate(flops=flops, bytes_accessed=moved, transcendentals=exps)


def shards(queries, kv_latent, key_rope, kv_gain, w_kv_up, prefix_len, page_owner, page_offset):
    toks = queries.shape[1]
    heads = queries.shape[2]
    n_seq = lax.axis_size("seq")
    n_dec = lax.axis_size("dec")
    chips = n_seq // 2
    length = toks * n_seq
    per = heads // n_seq
    cos, sin = rotation(length, toks)
    seq = jnp.reshape(lax.axis_index("seq"), (1,)).astype(jnp.int32)

    def along_x(a, k):
        return lax.ppermute(a, "seq", [(i, (i + 2 * k) % n_seq) for i in range(n_seq)])

    def partner(a):
        return lax.ppermute(a, "seq", [(i, i ^ 1) for i in range(n_seq)])

    w_left, w_right, w_far = (along_x(w_kv_up, k) for k in (1, -1, 2))

    q = jnp.transpose(queries[0], (1, 2, 0)).reshape(chips, 2, per * QK, toks)
    q_partner = partner(q)

    wide, tiles = pl.pallas_call(
        prepare,
        in_specs=[SMEM, SMEM] + [VMEM] * 5,
        out_specs=[VMEM, VMEM],
        out_shape=[
            jax.ShapeDtypeStruct((toks, WIDE), BF),
            jax.ShapeDtypeStruct((n_dec, ROWS, LANES), BF),
        ],
        cost_estimate=cost(500000, 800000),
        name="prepare",
    )(seq, prefix_len, kv_latent[0], key_rope[0].T, kv_gain, cos, sin)

    pairs = [[2 * i, 2 * i + 1] for i in range(chips)]
    chip_wide = lax.all_gather(wide, "seq", axis=0, axis_index_groups=pairs, tiled=True)
    all_wide = [chip_wide] + [along_x(chip_wide, k) for k in range(1, chips)]

    got = lax.all_to_all(tiles, "dec", split_axis=0, concat_axis=0, tiled=True)
    turned = pl.pallas_call(
        turn,
        in_specs=[SMEM, SMEM, VMEM],
        out_specs=VMEM,
        out_shape=jax.ShapeDtypeStruct((n_dec * MOST, ROWS, LANES), BF),
        cost_estimate=cost(0, 800000),
        name="turn",
    )(page_owner, page_offset, got)
    pool = lax.all_to_all(
        turned.reshape(n_dec, MOST, ROWS, LANES), "dec", split_axis=0, concat_axis=0, tiled=True
    )

    shape = [
        jax.ShapeDtypeStruct((toks, heads * VDIM), BF),
        jax.ShapeDtypeStruct((chips, toks, per * VDIM), BF),
    ]
    done = []
    for shifts, shard in (((0, chips - 1, 1), (w_kv_up, w_left, w_right)), ((2,), (w_far,))):
        n = len(shifts)
        given = (seq, prefix_len, q, q_partner, cos, sin, *all_wide, *shard)
        done = pl.pallas_call(
            functools.partial(attend, shifts, bool(done)),
            in_specs=[SMEM, SMEM, ANY, ANY, VMEM, VMEM] + [ANY] * (chips + n + len(done)),
            out_specs=[ANY, ANY],
            out_shape=shape,
            input_output_aliases={len(given) + i: i for i in range(len(done))},
            scratch_shapes=[
                pltpu.VMEM((2, chips, per * QK, toks), BF),
                pltpu.VMEM((length, LATENT), BF),
                pltpu.VMEM((length, 2 * ROPE), BF),
                pltpu.VMEM((n,) + w_kv_up.shape, BF),
                pltpu.VMEM((2, length, NOPE + 2 * ROPE), BF),
                pltpu.VMEM((2, length, VDIM), BF),
                pltpu.VMEM((2, 2 * toks, NOPE + 2 * ROPE), BF),
                pltpu.VMEM((n, 2, toks, per * VDIM), BF),
                pltpu.SemaphoreType.DMA((2,)),
                pltpu.SemaphoreType.DMA((2, chips)),
                pltpu.SemaphoreType.DMA((n,)),
                pltpu.SemaphoreType.DMA((n, 2)),
            ],
            compiler_params=pltpu.CompilerParams(vmem_limit_bytes=58 * 2**20),
            cost_estimate=cost(n * 2 * 10**9, n * 2 * 10**6, n * 10**6),
            name="attend",
        )(*given, *done)
    out, send = done
    back = partner(send)

    used = toks * (LATENT + ROPE) // (ROWS * LANES)
    attn_out, pool_lat, pool_rope = pl.pallas_call(
        finish,
        grid=(1,),
        in_specs=[
            SMEM,
            ANY,
            pl.BlockSpec((used, MOST, ROWS, LANES), lambda i: (0, 0, 0, 0)),
            ANY,
        ],
        out_specs=[ANY, VMEM, VMEM],
        out_shape=[
            shape[0],
            jax.ShapeDtypeStruct((MOST * toks, LATENT), BF),
            jax.ShapeDtypeStruct((ROPE, MOST * toks), BF),
        ],
        input_output_aliases={3: 0},
        scratch_shapes=[pltpu.SemaphoreType.DMA((chips,))],
        cost_estimate=cost(0, 2500000),
        name="finish",
    )(seq, back, pool, out)
    return attn_out[None], pool_lat[None], pool_rope.T[None]


def solution(mesh):
    return jax.shard_map(
        shards,
        mesh=mesh,
        in_specs=(
            P("dec", "seq", None, None),
            P("dec", "seq", None),
            P("dec", "seq", None),
            P(),
            P(None, "seq"),
            P("dec"),
            P(),
            P(),
        ),
        out_specs=(P("dec", "seq", None), P("dec", "seq", None), P("dec", "seq", None)),
        check_vma=False,
    )
```

```python
import functools

import jax
import jax.numpy as jnp
import numpy as np
from jax import lax
from jax.experimental import pallas as pl
from jax.experimental.pallas import tpu as pltpu
from jax.sharding import PartitionSpec as P

NOPE = 128
ROPE = 64
HALF = ROPE // 2
QK = NOPE + ROPE
VDIM = 128
LATENT = 512
PAGE = 16
MOST = 2
WIDE = LATENT + 2 * ROPE
ROWS = 16
LANES = 128
FAR = -1e30
BF = jnp.bfloat16
F32 = jnp.float32
VMEM = pl.BlockSpec(memory_space=pltpu.VMEM)
SMEM = pl.BlockSpec(memory_space=pltpu.SMEM)


def rotation(length, toks):
    freq = 50000.0 ** (-2.0 * np.arange(HALF, dtype=np.float64) / ROPE)
    angle = freq[:, None] * np.arange(length, dtype=np.float64)[None, :]
    angle = angle.reshape(HALF, length // toks, toks).transpose(1, 0, 2)
    return np.cos(angle).astype(np.float32), np.sin(angle).astype(np.float32)


def prepare(seq_ref, len_ref, lat_ref, rope_ref, gain_ref, cos_ref, sin_ref, wide_ref, tiles_ref):
    toks = lat_ref.shape[0]
    x = lat_ref[...].astype(F32)
    scale = lax.rsqrt(jnp.mean(x * x, axis=-1, keepdims=True) + 1e-06)
    lat = x * scale * gain_ref[...][None, :].astype(F32)
    a = rope_ref[:HALF].astype(F32)
    b = rope_ref[HALF:].astype(F32)
    c = cos_ref[seq_ref[0]]
    s = sin_ref[seq_ref[0]]
    rot = jnp.concatenate([a * c - b * s, b * c + a * s], axis=0)
    wide_ref[:, :LATENT] = lat.astype(BF)
    padded = jnp.concatenate([rot, jnp.zeros_like(rot)], axis=0)
    wide_ref[:, LATENT:] = padded.T.astype(BF)
    kept = PAGE * ((len_ref[0] + PAGE - 1) // PAGE) - seq_ref[0] * toks
    rows = lax.broadcasted_iota(jnp.int32, lat.shape, 0)
    lat = jnp.where(rows < kept, lat, 0.0).astype(BF)
    lanes = lax.broadcasted_iota(jnp.int32, rot.shape, 1)
    rot = jnp.where(lanes < kept, rot, 0.0).astype(BF)
    across = LATENT // LANES
    down = toks // ROWS
    for i in range(down):
        for j in range(across):
            tiles_ref[i * across + j] = lat[
                ROWS * i : ROWS * (i + 1), LANES * j : LANES * (j + 1)
            ]
    for i in range(ROPE // ROWS):
        tiles_ref[down * across + i] = rot[ROWS * i : ROWS * (i + 1)]
    used = down * across + ROPE // ROWS
    tiles_ref[used:] = jnp.zeros_like(tiles_ref[used:])


def turn(owner_ref, offset_ref, got_ref, o_ref):
    o_ref[...] = jnp.zeros_like(o_ref)
    for p in range(got_ref.shape[0]):
        o_ref[owner_ref[p] * MOST + offset_ref[p] // 8] = got_ref[p]


def attend(shifts, seq_ref, len_ref, q_ref, p_ref, cos_ref, sin_ref, *rest):
    chips = len(shifts)
    lat_refs, w_refs, rest = rest[:chips], rest[chips : 2 * chips + 1], rest[2 * chips + 1 :]
    own_ref, send_ref, lat_s, k_s, v_s, q_s, w_s = rest
    toks = q_ref.shape[3]
    pair = 2 * toks
    s = seq_ref[0]
    c = s % 2
    x = s // 2
    size = len_ref[0]
    scale = float(np.log2(np.e) / np.sqrt(QK))
    row = lax.broadcasted_iota(jnp.int32, (pair, 1), 0)
    pos = jnp.where(row < toks, c * toks + row, (1 - c) * toks + row - toks)
    causal = lax.broadcasted_iota(jnp.int32, (pair, pair), 1) <= pos
    alive = x * pair + pos < size
    heads = own_ref.shape[2] // VDIM
    slots = k_s.shape[0]

    def queries(n, chip, i):
        base = i * QK
        for j, (ref, block) in enumerate(((q_ref, s), (p_ref, s + 1 - 2 * c))):
            span = slice(j * toks, (j + 1) * toks)
            a = ref[chip, c, base + NOPE : base + NOPE + HALF].astype(F32)
            b = ref[chip, c, base + NOPE + HALF : base + QK].astype(F32)
            co = cos_ref[block]
            si = sin_ref[block]
            rot = [a * co - b * si, b * co + a * si, ones]
            q_s[n, span, :NOPE] = ref[chip, c, base : base + NOPE].T
            q_s[n, span, NOPE:] = jnp.concatenate(rot, axis=0).astype(BF).T

    lane = lax.broadcasted_iota(jnp.int32, (pair, 2 * ROPE), 1)
    for k in range(chips):
        rows = slice(k * pair, (k + 1) * pair)
        lat_s[rows] = lat_refs[k][:, :LATENT]
        tail = lat_refs[k][:, LATENT:]
        if k:
            bias = jnp.where(k <= x, 0.0, FAR)
            tail = jnp.where(lane == ROPE, bias, tail.astype(F32)).astype(BF)
        for n in range(slots):
            k_s[n, rows, NOPE:] = tail
    ones = (lax.broadcasted_iota(jnp.int32, (ROPE, toks), 0) == 0).astype(F32)
    depth = LATENT // 2
    for j in range(2):
        w_s[j * depth : (j + 1) * depth] = w_refs[chips - 1 + j][...]
    w_all = w_refs[: chips - 1] + (w_s,)
    for r in range(chips):
        chip = lax.rem(x + shifts[r], chips)
        for i in range(heads):
            n = (r * heads + i) % slots
            cols = slice(i * (NOPE + VDIM), (i + 1) * (NOPE + VDIM))
            kv = jnp.dot(
                lat_s[...], w_all[r][:, cols], preferred_element_type=F32
            )
            k_s[n, :, :NOPE] = kv[:, :NOPE].astype(BF)
            v_s[n] = kv[:, NOPE:].astype(BF)
            queries(n, chip, i)
            dots = lax.dot_general(
                q_s[n], k_s[n], (((1,), (1,)), ((), ())), preferred_element_type=F32
            )
            near = jnp.where(causal, dots[:, :pair], FAR)
            dots = jnp.concatenate([near, dots[:, pair:]], axis=1)
            top = jnp.max(dots, axis=1, keepdims=True)
            probs = jnp.exp2((dots - top) * scale)
            total = jnp.sum(probs, axis=1, keepdims=True)
            out = jnp.dot(probs.astype(BF), v_s[n], preferred_element_type=F32)
            out = jnp.where(alive, out / total, 0.0).astype(BF)
            own_ref[r, :, i * VDIM : (i + 1) * VDIM] = out[:toks]
            send_ref[r, :, i * VDIM : (i + 1) * VDIM] = out[toks:]


def finish(shifts, seq_ref, own_ref, back_ref, pool_ref, o_ref, lat_ref, rope_ref):
    chips, _, width = own_ref.shape
    s = seq_ref[0]
    c = s % 2
    for r, shift in enumerate(shifts):
        base = lax.rem(s // 2 + shift, chips) * 2 * width
        mine = pl.multiple_of(base + c * width, width)
        other = pl.multiple_of(base + (1 - c) * width, width)
        o_ref[:, pl.ds(mine, width)] = own_ref[r]
        o_ref[:, pl.ds(other, width)] = back_ref[r]
    toks = lat_ref.shape[0] // MOST
    across = LATENT // LANES
    down = toks // ROWS
    for m in range(MOST):
        for i in range(down):
            for j in range(across):
                t = i * across + j
                lat_ref[
                    m * toks + ROWS * i : m * toks + ROWS * (i + 1), LANES * j : LANES * (j + 1)
                ] = pool_ref[t, m]
        for i in range(ROPE // ROWS):
            t = down * across + i
            rope_ref[ROWS * i : ROWS * (i + 1), m * toks : (m + 1) * toks] = pool_ref[t, m]


def cost(flops, moved, exps=0):
    return pl.CostEstimate(flops=flops, bytes_accessed=moved, transcendentals=exps)


def shards(queries, kv_latent, key_rope, kv_gain, w_kv_up, prefix_len, page_owner, page_offset):
    toks = queries.shape[1]
    heads = queries.shape[2]
    n_seq = lax.axis_size("seq")
    n_dec = lax.axis_size("dec")
    chips = n_seq // 2
    length = toks * n_seq
    per = heads // n_seq
    cos, sin = rotation(length, toks)
    seq = jnp.reshape(lax.axis_index("seq"), (1,)).astype(jnp.int32)

    def along_x(a, k):
        return lax.ppermute(a, "seq", [(i, (i + 2 * k) % n_seq) for i in range(n_seq)])

    def partner(a):
        return lax.ppermute(a, "seq", [(i, i ^ 1) for i in range(n_seq)])

    w_left = along_x(w_kv_up, 1)
    w_right = along_x(w_kv_up, -1)
    q = jnp.transpose(queries[0], (1, 2, 0)).reshape(chips, 2, per * QK, toks)
    q_partner = partner(q)

    wide, tiles = pl.pallas_call(
        prepare,
        in_specs=[SMEM, SMEM] + [VMEM] * 5,
        out_specs=[VMEM, VMEM],
        out_shape=[
            jax.ShapeDtypeStruct((toks, WIDE), BF),
            jax.ShapeDtypeStruct((n_dec, ROWS, LANES), BF),
        ],
        cost_estimate=cost(500000, 800000),
        name="prepare",
    )(seq, prefix_len, kv_latent[0], key_rope[0].T, kv_gain, cos, sin)

    pairs = [[2 * i, 2 * i + 1] for i in range(chips)]
    chip_wide = lax.all_gather(wide, "seq", axis=0, axis_index_groups=pairs, tiled=True)
    all_wide = [chip_wide] + [along_x(chip_wide, k) for k in range(1, chips)]

    got = lax.all_to_all(tiles, "dec", split_axis=0, concat_axis=0, tiled=True)
    got, w_left, w_right, all_wide = lax.optimization_barrier((got, w_left, w_right, all_wide))
    depth = LATENT // 2
    w_far = (along_x(w_left[:depth], 1), along_x(w_right[depth:], -1))
    turned = pl.pallas_call(
        turn,
        in_specs=[SMEM, SMEM, VMEM],
        out_specs=VMEM,
        out_shape=jax.ShapeDtypeStruct((n_dec * MOST, ROWS, LANES), BF),
        cost_estimate=cost(0, 800000),
        name="turn",
    )(page_owner, page_offset, got)
    pool = lax.all_to_all(
        turned.reshape(n_dec, MOST, ROWS, LANES), "dec", split_axis=0, concat_axis=0, tiled=True
    )

    shifts = (0, chips - 1, 1, 2)
    own, send = pl.pallas_call(
        functools.partial(attend, shifts),
        in_specs=[SMEM, SMEM] + [VMEM] * (4 + 2 * chips + 1),
        out_specs=[VMEM, VMEM],
        out_shape=[jax.ShapeDtypeStruct((chips, toks, per * VDIM), BF)] * 2,
        scratch_shapes=[
            pltpu.VMEM((length, LATENT), BF),
            pltpu.VMEM((2, length, NOPE + 2 * ROPE), BF),
            pltpu.VMEM((2, length, VDIM), BF),
            pltpu.VMEM((2, 2 * toks, NOPE + 2 * ROPE), BF),
            pltpu.VMEM(w_kv_up.shape, BF),
        ],
        compiler_params=pltpu.CompilerParams(vmem_limit_bytes=32 * 2**20),
        cost_estimate=cost(8 * 10**9, 8 * 10**6, 4 * 10**6),
        name="attend",
    )(seq, prefix_len, q, q_partner, cos, sin, *all_wide, w_kv_up, w_left, w_right, *w_far)
    back = partner(send)

    used = toks * (LATENT + ROPE) // (ROWS * LANES)
    attn_out, pool_lat, pool_rope = pl.pallas_call(
        functools.partial(finish, shifts),
        grid=(1,),
        in_specs=[
            SMEM,
            VMEM,
            VMEM,
            pl.BlockSpec((used, MOST, ROWS, LANES), lambda i: (0, 0, 0, 0)),
        ],
        out_specs=[VMEM, VMEM, VMEM],
        out_shape=[
            jax.ShapeDtypeStruct((toks, heads * VDIM), BF),
            jax.ShapeDtypeStruct((MOST * toks, LATENT), BF),
            jax.ShapeDtypeStruct((ROPE, MOST * toks), BF),
        ],
        cost_estimate=cost(0, 2500000),
        name="finish",
    )(seq, own, back, pool)
    return attn_out[None], pool_lat[None], pool_rope.T[None]


def solution(mesh):
    return jax.shard_map(
        shards,
        mesh=mesh,
        in_specs=(
            P("dec", "seq", None, None),
            P("dec", "seq", None),
            P("dec", "seq", None),
            P(),
            P(None, "seq"),
            P("dec"),
            P(),
            P(),
        ),
        out_specs=(P("dec", "seq", None), P("dec", "seq", None), P("dec", "seq", None)),
        check_vma=False,
    )
```

```python
import functools

import jax
import jax.numpy as jnp
import numpy as np
from jax import lax
from jax.experimental import pallas as pl
from jax.experimental.pallas import tpu as pltpu
from jax.sharding import PartitionSpec as P

NOPE = 128
ROPE = 64
HALF = ROPE // 2
QK = NOPE + ROPE
VDIM = 128
LATENT = 512
PAGE = 16
MOST = 2
WIDE = LATENT + 2 * ROPE
ROWS = 16
LANES = 128
FAR = -1e30
BF = jnp.bfloat16
F32 = jnp.float32
VMEM = pl.BlockSpec(memory_space=pltpu.VMEM)
SMEM = pl.BlockSpec(memory_space=pltpu.SMEM)
ANY = pl.BlockSpec(memory_space=pl.ANY)


def rotation(length, toks):
    freq = 50000.0 ** (-2.0 * np.arange(HALF, dtype=np.float64) / ROPE)
    angle = freq[:, None] * np.arange(length, dtype=np.float64)[None, :]
    angle = angle.reshape(HALF, length // toks, toks).transpose(1, 0, 2)
    return np.cos(angle).astype(np.float32), np.sin(angle).astype(np.float32)


def prepare(seq_ref, len_ref, lat_ref, rope_ref, gain_ref, cos_ref, sin_ref, wide_ref, tiles_ref):
    toks = lat_ref.shape[0]
    x = lat_ref[...].astype(F32)
    scale = lax.rsqrt(jnp.mean(x * x, axis=-1, keepdims=True) + 1e-06)
    lat = x * scale * gain_ref[...][None, :].astype(F32)
    a = rope_ref[:HALF].astype(F32)
    b = rope_ref[HALF:].astype(F32)
    c = cos_ref[seq_ref[0]]
    s = sin_ref[seq_ref[0]]
    rot = jnp.concatenate([a * c - b * s, b * c + a * s], axis=0)
    wide_ref[:, :LATENT] = lat.astype(BF)
    padded = jnp.concatenate([rot, jnp.zeros_like(rot)], axis=0)
    wide_ref[:, LATENT:] = padded.T.astype(BF)
    kept = PAGE * ((len_ref[0] + PAGE - 1) // PAGE) - seq_ref[0] * toks
    rows = lax.broadcasted_iota(jnp.int32, lat.shape, 0)
    lat = jnp.where(rows < kept, lat, 0.0).astype(BF)
    lanes = lax.broadcasted_iota(jnp.int32, rot.shape, 1)
    rot = jnp.where(lanes < kept, rot, 0.0).astype(BF)
    across = LATENT // LANES
    down = toks // ROWS
    for i in range(down):
        for j in range(across):
            tiles_ref[i * across + j] = lat[
                ROWS * i : ROWS * (i + 1), LANES * j : LANES * (j + 1)
            ]
    for i in range(ROPE // ROWS):
        tiles_ref[down * across + i] = rot[ROWS * i : ROWS * (i + 1)]
    used = down * across + ROPE // ROWS
    tiles_ref[used:] = jnp.zeros_like(tiles_ref[used:])


def pack(w_ref, wide_ref, o_ref):
    rows = wide_ref.shape[0]
    depth = w_ref.shape[0]
    half = rows // 2
    o_ref[:depth] = w_ref[...]
    for j in range(2):
        o_ref[depth : depth + half, j * LATENT : (j + 1) * LATENT] = wide_ref[
            j * half : (j + 1) * half, :LATENT
        ]
    step = rows // 8
    for j in range(8):
        o_ref[depth + half :, j * 2 * ROPE : (j + 1) * 2 * ROPE] = wide_ref[
            j * step : (j + 1) * step, LATENT:
        ]


def turn(owner_ref, offset_ref, got_ref, o_ref):
    o_ref[...] = jnp.zeros_like(o_ref)
    for p in range(got_ref.shape[0]):
        o_ref[owner_ref[p] * MOST + offset_ref[p] // 8] = got_ref[p]


def unpack(a_ref, lat_ref, rope_ref):
    toks = lat_ref.shape[0] // MOST
    across = LATENT // LANES
    down = toks // ROWS
    for m in range(MOST):
        for i in range(down):
            for j in range(across):
                lat_ref[
                    m * toks + ROWS * i : m * toks + ROWS * (i + 1), LANES * j : LANES * (j + 1)
                ] = a_ref[i * across + j, m]
        for i in range(ROPE // ROWS):
            rope_ref[ROWS * i : ROWS * (i + 1), m * toks : (m + 1) * toks] = a_ref[
                down * across + i, m
            ]


def attend(shifts, before, seq_ref, len_ref, q_ref, p_ref, cos_ref, sin_ref, *rest):
    packs, far_ref, rest = rest[:3], rest[3], rest[4:]
    if before:
        w_refs, old_ref, rest = rest[:2], rest[2], rest[3:]
    own_ref, send_ref, lat_s, k_s, v_s, q_s, w_s, p_s, p_sem = rest
    chips = q_ref.shape[0]
    count = len(shifts)
    toks = q_ref.shape[3]
    pair = 2 * toks
    s = seq_ref[0]
    c = s % 2
    x = s // 2
    copies = [
        pltpu.make_async_copy(p_ref.at[lax.rem(x + shifts[r], chips), c], p_s.at[r], p_sem.at[r])
        for r in range(count)
    ]
    for copy in copies:
        copy.start()
    if before:
        send_ref[:before] = old_ref[...]
    size = len_ref[0]
    scale = float(np.log2(np.e) / np.sqrt(QK))
    row = lax.broadcasted_iota(jnp.int32, (pair, 1), 0)
    pos = jnp.where(row < toks, c * toks + row, (1 - c) * toks + row - toks)
    causal = lax.broadcasted_iota(jnp.int32, (pair, pair), 1) <= pos
    alive = x * pair + pos < size
    heads = own_ref.shape[2] // VDIM
    slots = k_s.shape[0]

    def queries(n, r, chip, i):
        base = i * QK
        for j, (ref, block) in enumerate(((q_ref.at[chip, c], s), (p_s.at[r], s + 1 - 2 * c))):
            span = slice(j * toks, (j + 1) * toks)
            a = ref[base + NOPE : base + NOPE + HALF].astype(F32)
            b = ref[base + NOPE + HALF : base + QK].astype(F32)
            co = cos_ref[block]
            si = sin_ref[block]
            rot = [a * co - b * si, b * co + a * si, ones]
            q_s[n, span, :NOPE] = ref[base : base + NOPE].T
            q_s[n, span, NOPE:] = jnp.concatenate(rot, axis=0).astype(BF).T

    depth = LATENT
    for k, ref in enumerate((packs[0], packs[1], far_ref, packs[2])):
        bias = jnp.where(k <= x, 0.0, FAR)
        step = pair // 8
        for j in range(8):
            rows = slice(k * pair + j * step, k * pair + (j + 1) * step)
            if k == 2:
                tail = ref[j * step : (j + 1) * step, LATENT:]
            else:
                tail = ref[depth + toks :, j * 2 * ROPE : (j + 1) * 2 * ROPE]
            if k:
                lane = lax.broadcasted_iota(jnp.int32, tail.shape, 1)
                tail = jnp.where(lane == ROPE, bias, tail.astype(F32)).astype(BF)
            for n in range(slots):
                k_s[n, rows, NOPE:] = tail
        if k == 2:
            lat_s[k * pair : (k + 1) * pair] = ref[:, :LATENT]
        else:
            for j in range(2):
                lat_s[k * pair + j * toks : k * pair + (j + 1) * toks] = ref[
                    depth : depth + toks, j * LATENT : (j + 1) * LATENT
                ]
    if before:
        for j in range(2):
            w_s[j * depth // 2 : (j + 1) * depth // 2] = w_refs[j][...]
        shards = [w_s]
    else:
        shards = packs
    ones = (lax.broadcasted_iota(jnp.int32, (ROPE, toks), 0) == 0).astype(F32)
    for r in range(count):
        chip = lax.rem(x + shifts[r], chips)
        for i in range(heads):
            n = (r * heads + i) % slots
            cols = slice(i * (NOPE + VDIM), (i + 1) * (NOPE + VDIM))
            kv = jnp.dot(
                lat_s[...], shards[r][:depth, cols], preferred_element_type=F32
            )
            k_s[n, :, :NOPE] = kv[:, :NOPE].astype(BF)
            v_s[n] = kv[:, NOPE:].astype(BF)
            if i == 0:
                copies[r].wait()
            queries(n, r, chip, i)
            dots = lax.dot_general(
                q_s[n], k_s[n], (((1,), (1,)), ((), ())), preferred_element_type=F32
            )
            near = jnp.where(causal, dots[:, :pair], FAR)
            dots = jnp.concatenate([near, dots[:, pair:]], axis=1)
            top = jnp.max(dots, axis=1, keepdims=True)
            probs = jnp.exp2((dots - top) * scale)
            total = jnp.sum(probs, axis=1, keepdims=True)
            out = jnp.dot(probs.astype(BF), v_s[n], preferred_element_type=F32)
            out = jnp.where(alive, out / total, 0.0).astype(BF)
            own_ref[r, :, i * VDIM : (i + 1) * VDIM] = out[:toks]
            send_ref[before + r, :, i * VDIM : (i + 1) * VDIM] = out[toks:]


def lay_out(shifts, seq_ref, near_ref, far_ref, back_ref, o_ref):
    chips, _, width = back_ref.shape
    near = near_ref.shape[0]
    s = seq_ref[0]
    c = s % 2
    for r, shift in enumerate(shifts):
        base = lax.rem(s // 2 + shift, chips) * 2 * width
        mine = pl.multiple_of(base + c * width, width)
        other = pl.multiple_of(base + (1 - c) * width, width)
        o_ref[:, pl.ds(mine, width)] = near_ref[r] if r < near else far_ref[r - near]
        o_ref[:, pl.ds(other, width)] = back_ref[r]


def cost(flops, moved, exps=0):
    return pl.CostEstimate(flops=flops, bytes_accessed=moved, transcendentals=exps)


def shards(queries, kv_latent, key_rope, kv_gain, w_kv_up, prefix_len, page_owner, page_offset):
    toks = queries.shape[1]
    heads = queries.shape[2]
    n_seq = lax.axis_size("seq")
    n_dec = lax.axis_size("dec")
    chips = n_seq // 2
    length = toks * n_seq
    per = heads // n_seq
    cos, sin = rotation(length, toks)
    seq = jnp.reshape(lax.axis_index("seq"), (1,)).astype(jnp.int32)

    def along_x(a, k):
        return lax.ppermute(a, "seq", [(i, (i + 2 * k) % n_seq) for i in range(n_seq)])

    def partner(a):
        return lax.ppermute(a, "seq", [(i, i ^ 1) for i in range(n_seq)])

    q = jnp.transpose(queries[0], (1, 2, 0)).reshape(chips, 2, per * QK, toks)
    q_partner = partner(q)

    wide, tiles = pl.pallas_call(
        prepare,
        in_specs=[SMEM, SMEM] + [VMEM] * 5,
        out_specs=[VMEM, VMEM],
        out_shape=[
            jax.ShapeDtypeStruct((toks, WIDE), BF),
            jax.ShapeDtypeStruct((n_dec, ROWS, LANES), BF),
        ],
        cost_estimate=cost(500000, 800000),
        name="prepare",
    )(seq, prefix_len, kv_latent[0], key_rope[0].T, kv_gain, cos, sin)

    pairs = [[2 * i, 2 * i + 1] for i in range(chips)]
    chip_wide = lax.all_gather(wide, "seq", axis=0, axis_index_groups=pairs, tiled=True)
    far_wide = along_x(chip_wide, 2)
    here = pl.pallas_call(
        pack,
        in_specs=[VMEM, VMEM],
        out_specs=VMEM,
        out_shape=jax.ShapeDtypeStruct((LATENT + toks + toks // 4, w_kv_up.shape[1]), BF),
        cost_estimate=cost(0, 4000000),
        name="pack",
    )(w_kv_up, chip_wide)
    left, right = along_x(here, 1), along_x(here, -1)
    depth = LATENT // 2
    w_far = (along_x(left[:depth], 1), along_x(right[depth : 2 * depth], -1))

    tiles, here = lax.optimization_barrier((tiles, here))
    got = lax.all_to_all(tiles, "dec", split_axis=0, concat_axis=0, tiled=True)
    turned = pl.pallas_call(
        turn,
        in_specs=[SMEM, SMEM, VMEM],
        out_specs=VMEM,
        out_shape=jax.ShapeDtypeStruct((n_dec * MOST, ROWS, LANES), BF),
        cost_estimate=cost(0, 800000),
        name="turn",
    )(page_owner, page_offset, got)
    pool = lax.all_to_all(
        turned.reshape(n_dec, MOST, ROWS, LANES), "dec", split_axis=0, concat_axis=0, tiled=True
    )

    shifts = (0, chips - 1, 1, 2)
    near = chips - 1
    packs = (here, left, right, far_wide)
    own, more = [], ()
    for first, last in ((0, near), (near, chips)):
        n = last - first
        heads_of = jax.ShapeDtypeStruct((n, toks, per * VDIM), BF)
        a, b = pl.pallas_call(
            functools.partial(attend, shifts[first:last], first),
            in_specs=[SMEM, SMEM, VMEM, ANY] + [VMEM] * (2 + len(packs) + len(more)),
            out_specs=[VMEM, VMEM],
            out_shape=[heads_of, jax.ShapeDtypeStruct((last, toks, per * VDIM), BF)],
            scratch_shapes=[
                pltpu.VMEM((length, LATENT), BF),
                pltpu.VMEM((2, length, NOPE + 2 * ROPE), BF),
                pltpu.VMEM((2, length, VDIM), BF),
                pltpu.VMEM((2, 2 * toks, NOPE + 2 * ROPE), BF),
                pltpu.VMEM(w_kv_up.shape, BF),
                pltpu.VMEM((n, per * QK, toks), BF),
                pltpu.SemaphoreType.DMA((n,)),
            ],
            compiler_params=pltpu.CompilerParams(vmem_limit_bytes=36 * 2**20),
            cost_estimate=cost(n * 2 * 10**9, n * 10**6, n * 10**6),
            name="attend",
        )(seq, prefix_len, q, q_partner, cos, sin, *packs, *more)
        own.append(a)
        more = (*w_far, b)
    back = partner(b)

    attn_out = pl.pallas_call(
        functools.partial(lay_out, shifts),
        in_specs=[SMEM] + [VMEM] * 3,
        out_specs=VMEM,
        out_shape=jax.ShapeDtypeStruct((toks, heads * VDIM), BF),
        cost_estimate=cost(0, 2000000),
        name="lay_out",
    )(seq, *own, back)

    pool_lat, pool_rope = pl.pallas_call(
        unpack,
        in_specs=[VMEM],
        out_specs=[VMEM, VMEM],
        out_shape=[
            jax.ShapeDtypeStruct((MOST * toks, LATENT), BF),
            jax.ShapeDtypeStruct((ROPE, MOST * toks), BF),
        ],
        cost_estimate=cost(0, 600000),
        name="unpack",
    )(pool)
    return attn_out[None], pool_lat[None], pool_rope.T[None]


def solution(mesh):
    return jax.shard_map(
        shards,
        mesh=mesh,
        in_specs=(
            P("dec", "seq", None, None),
            P("dec", "seq", None),
            P("dec", "seq", None),
            P(),
            P(None, "seq"),
            P("dec"),
            P(),
            P(),
        ),
        out_specs=(P("dec", "seq", None), P("dec", "seq", None), P("dec", "seq", None)),
        check_vma=False,
    )
```

```python
import functools

import jax
import jax.numpy as jnp
import numpy as np
from jax import lax
from jax.experimental import pallas as pl
from jax.experimental.pallas import tpu as pltpu
from jax.sharding import PartitionSpec as P

NOPE = 128
ROPE = 64
HALF = ROPE // 2
QK = NOPE + ROPE
VDIM = 128
LATENT = 512
PAGE = 16
MOST = 2
WIDE = LATENT + 2 * ROPE
ROWS = 16
LANES = 128
FAR = -1e30
BF = jnp.bfloat16
F32 = jnp.float32
VMEM = pl.BlockSpec(memory_space=pltpu.VMEM)
SMEM = pl.BlockSpec(memory_space=pltpu.SMEM)


def rotation(length, toks):
    freq = 50000.0 ** (-2.0 * np.arange(HALF, dtype=np.float64) / ROPE)
    angle = freq[:, None] * np.arange(length, dtype=np.float64)[None, :]
    angle = angle.reshape(HALF, length // toks, toks).transpose(1, 0, 2)
    return np.cos(angle).astype(np.float32), np.sin(angle).astype(np.float32)


def prepare(seq_ref, len_ref, lat_ref, rope_ref, gain_ref, cos_ref, sin_ref, wide_ref, tiles_ref):
    toks = lat_ref.shape[0]
    x = lat_ref[...].astype(F32)
    scale = lax.rsqrt(jnp.mean(x * x, axis=-1, keepdims=True) + 1e-06)
    lat = x * scale * gain_ref[...][None, :].astype(F32)
    a = rope_ref[:HALF].astype(F32)
    b = rope_ref[HALF:].astype(F32)
    c = cos_ref[seq_ref[0]]
    s = sin_ref[seq_ref[0]]
    rot = jnp.concatenate([a * c - b * s, b * c + a * s], axis=0)
    wide_ref[:, :LATENT] = lat.astype(BF)
    padded = jnp.concatenate([rot, jnp.zeros_like(rot)], axis=0)
    wide_ref[:, LATENT:] = padded.T.astype(BF)
    kept = PAGE * ((len_ref[0] + PAGE - 1) // PAGE) - seq_ref[0] * toks
    rows = lax.broadcasted_iota(jnp.int32, lat.shape, 0)
    lat = jnp.where(rows < kept, lat, 0.0).astype(BF)
    lanes = lax.broadcasted_iota(jnp.int32, rot.shape, 1)
    rot = jnp.where(lanes < kept, rot, 0.0).astype(BF)
    across = LATENT // LANES
    down = toks // ROWS
    for i in range(down):
        for j in range(across):
            tiles_ref[i * across + j] = lat[
                ROWS * i : ROWS * (i + 1), LANES * j : LANES * (j + 1)
            ]
    for i in range(ROPE // ROWS):
        tiles_ref[down * across + i] = rot[ROWS * i : ROWS * (i + 1)]
    used = down * across + ROPE // ROWS
    tiles_ref[used:] = jnp.zeros_like(tiles_ref[used:])


def turn(owner_ref, offset_ref, got_ref, o_ref):
    o_ref[...] = jnp.zeros_like(o_ref)
    for p in range(got_ref.shape[0]):
        o_ref[owner_ref[p] * MOST + offset_ref[p] // 8] = got_ref[p]


def unpack(a_ref, lat_ref, rope_ref):
    toks = lat_ref.shape[0] // MOST
    across = LATENT // LANES
    down = toks // ROWS
    for m in range(MOST):
        for i in range(down):
            for j in range(across):
                lat_ref[
                    m * toks + ROWS * i : m * toks + ROWS * (i + 1), LANES * j : LANES * (j + 1)
                ] = a_ref[i * across + j, m]
        for i in range(ROPE // ROWS):
            rope_ref[ROWS * i : ROWS * (i + 1), m * toks : (m + 1) * toks] = a_ref[
                down * across + i, m
            ]


def attend(shifts, seq_ref, len_ref, q_ref, p_ref, cos_ref, sin_ref, *rest):
    chips = len(shifts)
    lat_refs, w_refs, rest = rest[:chips], rest[chips : 2 * chips], rest[2 * chips :]
    own_ref, send_ref, lat_s, k_s, v_s, q_s = rest
    toks = q_ref.shape[3]
    pair = 2 * toks
    s = seq_ref[0]
    c = s % 2
    x = s // 2
    size = len_ref[0]
    scale = float(np.log2(np.e) / np.sqrt(QK))
    row = lax.broadcasted_iota(jnp.int32, (pair, 1), 0)
    pos = jnp.where(row < toks, c * toks + row, (1 - c) * toks + row - toks)
    causal = lax.broadcasted_iota(jnp.int32, (pair, pair), 1) <= pos
    alive = x * pair + pos < size
    heads = own_ref.shape[2] // VDIM
    slots = k_s.shape[0]

    def queries(n, chip, i):
        base = i * QK
        for j, (ref, block) in enumerate(((q_ref, s), (p_ref, s + 1 - 2 * c))):
            span = slice(j * toks, (j + 1) * toks)
            a = ref[chip, c, base + NOPE : base + NOPE + HALF].astype(F32)
            b = ref[chip, c, base + NOPE + HALF : base + QK].astype(F32)
            co = cos_ref[block]
            si = sin_ref[block]
            rot = [a * co - b * si, b * co + a * si, ones]
            q_s[n, span, :NOPE] = ref[chip, c, base : base + NOPE].T
            q_s[n, span, NOPE:] = jnp.concatenate(rot, axis=0).astype(BF).T

    lane = lax.broadcasted_iota(jnp.int32, (pair, 2 * ROPE), 1)
    for k in range(chips):
        rows = slice(k * pair, (k + 1) * pair)
        lat_s[rows] = lat_refs[k][:, :LATENT]
        tail = lat_refs[k][:, LATENT:]
        if k:
            bias = jnp.where(k <= x, 0.0, FAR)
            tail = jnp.where(lane == ROPE, bias, tail.astype(F32)).astype(BF)
        for n in range(slots):
            k_s[n, rows, NOPE:] = tail
    ones = (lax.broadcasted_iota(jnp.int32, (ROPE, toks), 0) == 0).astype(F32)
    for r in range(chips):
        chip = lax.rem(x + shifts[r], chips)
        for i in range(heads):
            n = (r * heads + i) % slots
            cols = slice(i * (NOPE + VDIM), (i + 1) * (NOPE + VDIM))
            kv = jnp.dot(
                lat_s[...], w_refs[r][:, cols], preferred_element_type=F32
            )
            k_s[n, :, :NOPE] = kv[:, :NOPE].astype(BF)
            v_s[n] = kv[:, NOPE:].astype(BF)
            queries(n, chip, i)
            dots = lax.dot_general(
                q_s[n], k_s[n], (((1,), (1,)), ((), ())), preferred_element_type=F32
            )
            near = jnp.where(causal, dots[:, :pair], FAR)
            dots = jnp.concatenate([near, dots[:, pair:]], axis=1)
            top = jnp.max(dots, axis=1, keepdims=True)
            probs = jnp.exp2((dots - top) * scale)
            total = jnp.sum(probs, axis=1, keepdims=True)
            out = jnp.dot(probs.astype(BF), v_s[n], preferred_element_type=F32)
            out = jnp.where(alive, out / total, 0.0).astype(BF)
            own_ref[r, :, i * VDIM : (i + 1) * VDIM] = out[:toks]
            send_ref[r, :, i * VDIM : (i + 1) * VDIM] = out[toks:]


def lay_out(shifts, seq_ref, own_ref, back_ref, o_ref):
    chips, _, width = own_ref.shape
    s = seq_ref[0]
    c = s % 2
    for r, shift in enumerate(shifts):
        base = lax.rem(s // 2 + shift, chips) * 2 * width
        mine = pl.multiple_of(base + c * width, width)
        other = pl.multiple_of(base + (1 - c) * width, width)
        o_ref[:, pl.ds(mine, width)] = own_ref[r]
        o_ref[:, pl.ds(other, width)] = back_ref[r]


def cost(flops, moved, exps=0):
    return pl.CostEstimate(flops=flops, bytes_accessed=moved, transcendentals=exps)


def shards(queries, kv_latent, key_rope, kv_gain, w_kv_up, prefix_len, page_owner, page_offset):
    toks = queries.shape[1]
    heads = queries.shape[2]
    n_seq = lax.axis_size("seq")
    n_dec = lax.axis_size("dec")
    chips = n_seq // 2
    length = toks * n_seq
    per = heads // n_seq
    cos, sin = rotation(length, toks)
    seq = jnp.reshape(lax.axis_index("seq"), (1,)).astype(jnp.int32)

    def along_x(a, k):
        return lax.ppermute(a, "seq", [(i, (i + 2 * k) % n_seq) for i in range(n_seq)])

    def partner(a):
        return lax.ppermute(a, "seq", [(i, i ^ 1) for i in range(n_seq)])

    w_left, w_right, w_far = (along_x(w_kv_up, k) for k in (1, -1, 2))

    q = jnp.transpose(queries[0], (1, 2, 0)).reshape(chips, 2, per * QK, toks)
    q_partner = partner(q)
    q_partner, kv_latent = lax.optimization_barrier((q_partner, kv_latent))

    wide, tiles = pl.pallas_call(
        prepare,
        in_specs=[SMEM, SMEM] + [VMEM] * 5,
        out_specs=[VMEM, VMEM],
        out_shape=[
            jax.ShapeDtypeStruct((toks, WIDE), BF),
            jax.ShapeDtypeStruct((n_dec, ROWS, LANES), BF),
        ],
        cost_estimate=cost(500000, 800000),
        name="prepare",
    )(seq, prefix_len, kv_latent[0], key_rope[0].T, kv_gain, cos, sin)

    pairs = [[2 * i, 2 * i + 1] for i in range(chips)]
    chip_wide = lax.all_gather(wide, "seq", axis=0, axis_index_groups=pairs, tiled=True)
    all_wide = [chip_wide] + [along_x(chip_wide, k) for k in range(1, chips)]

    got = lax.all_to_all(tiles, "dec", split_axis=0, concat_axis=0, tiled=True)
    turned = pl.pallas_call(
        turn,
        in_specs=[SMEM, SMEM, VMEM],
        out_specs=VMEM,
        out_shape=jax.ShapeDtypeStruct((n_dec * MOST, ROWS, LANES), BF),
        cost_estimate=cost(0, 800000),
        name="turn",
    )(page_owner, page_offset, got)
    pool = lax.all_to_all(
        turned.reshape(n_dec, MOST, ROWS, LANES), "dec", split_axis=0, concat_axis=0, tiled=True
    )

    shifts = (0, chips - 1, 1, 2)
    own, send = pl.pallas_call(
        functools.partial(attend, shifts),
        in_specs=[SMEM, SMEM] + [VMEM] * (4 + 2 * chips),
        out_specs=[VMEM, VMEM],
        out_shape=[jax.ShapeDtypeStruct((chips, toks, per * VDIM), BF)] * 2,
        scratch_shapes=[
            pltpu.VMEM((length, LATENT), BF),
            pltpu.VMEM((2, length, NOPE + 2 * ROPE), BF),
            pltpu.VMEM((2, length, VDIM), BF),
            pltpu.VMEM((2, 2 * toks, NOPE + 2 * ROPE), BF),
        ],
        compiler_params=pltpu.CompilerParams(vmem_limit_bytes=36 * 2**20),
        cost_estimate=cost(8 * 10**9, 8 * 10**6, 4 * 10**6),
        name="attend",
    )(seq, prefix_len, q, q_partner, cos, sin, *all_wide, w_kv_up, w_left, w_right, w_far)
    back = partner(send)

    attn_out = pl.pallas_call(
        functools.partial(lay_out, shifts),
        in_specs=[SMEM] + [VMEM] * 2,
        out_specs=VMEM,
        out_shape=jax.ShapeDtypeStruct((toks, heads * VDIM), BF),
        cost_estimate=cost(0, 2000000),
        name="lay_out",
    )(seq, own, back)

    pool_lat, pool_rope = pl.pallas_call(
        unpack,
        in_specs=[VMEM],
        out_specs=[VMEM, VMEM],
        out_shape=[
            jax.ShapeDtypeStruct((MOST * toks, LATENT), BF),
            jax.ShapeDtypeStruct((ROPE, MOST * toks), BF),
        ],
        cost_estimate=cost(0, 600000),
        name="unpack",
    )(pool)
    return attn_out[None], pool_lat[None], pool_rope.T[None]


def solution(mesh):
    return jax.shard_map(
        shards,
        mesh=mesh,
        in_specs=(
            P("dec", "seq", None, None),
            P("dec", "seq", None),
            P("dec", "seq", None),
            P(),
            P(None, "seq"),
            P("dec"),
            P(),
            P(),
        ),
        out_specs=(P("dec", "seq", None), P("dec", "seq", None), P("dec", "seq", None)),
        check_vma=False,
    )
```

```python
import functools

import jax
import jax.numpy as jnp
import numpy as np
from jax import lax
from jax.experimental import pallas as pl
from jax.experimental.pallas import tpu as pltpu
from jax.sharding import PartitionSpec as P

NOPE = 128
ROPE = 64
HALF = ROPE // 2
QK = NOPE + ROPE
VDIM = 128
LATENT = 512
PAGE = 16
MOST = 2
WIDE = LATENT + 2 * ROPE
ROWS = 16
LANES = 128
FAR = -1e30
BF = jnp.bfloat16
F32 = jnp.float32
VMEM = pl.BlockSpec(memory_space=pltpu.VMEM)
SMEM = pl.BlockSpec(memory_space=pltpu.SMEM)


def rotation(length, toks):
    freq = 50000.0 ** (-2.0 * np.arange(HALF, dtype=np.float64) / ROPE)
    angle = freq[:, None] * np.arange(length, dtype=np.float64)[None, :]
    angle = angle.reshape(HALF, length // toks, toks).transpose(1, 0, 2)
    return np.cos(angle).astype(np.float32), np.sin(angle).astype(np.float32)


def prepare(seq_ref, len_ref, lat_ref, rope_ref, gain_ref, cos_ref, sin_ref, wide_ref, tiles_ref):
    toks = lat_ref.shape[0]
    x = lat_ref[...].astype(F32)
    scale = lax.rsqrt(jnp.mean(x * x, axis=-1, keepdims=True) + 1e-06)
    lat = x * scale * gain_ref[...][None, :].astype(F32)
    a = rope_ref[:HALF].astype(F32)
    b = rope_ref[HALF:].astype(F32)
    c = cos_ref[seq_ref[0]]
    s = sin_ref[seq_ref[0]]
    rot = jnp.concatenate([a * c - b * s, b * c + a * s], axis=0)
    wide_ref[:, :LATENT] = lat.astype(BF)
    padded = jnp.concatenate([rot, jnp.zeros_like(rot)], axis=0)
    wide_ref[:, LATENT:] = padded.T.astype(BF)
    kept = PAGE * ((len_ref[0] + PAGE - 1) // PAGE) - seq_ref[0] * toks
    rows = lax.broadcasted_iota(jnp.int32, lat.shape, 0)
    lat = jnp.where(rows < kept, lat, 0.0).astype(BF)
    lanes = lax.broadcasted_iota(jnp.int32, rot.shape, 1)
    rot = jnp.where(lanes < kept, rot, 0.0).astype(BF)
    across = LATENT // LANES
    down = toks // ROWS
    for i in range(down):
        for j in range(across):
            tiles_ref[i * across + j] = lat[
                ROWS * i : ROWS * (i + 1), LANES * j : LANES * (j + 1)
            ]
    for i in range(ROPE // ROWS):
        tiles_ref[down * across + i] = rot[ROWS * i : ROWS * (i + 1)]
    used = down * across + ROPE // ROWS
    tiles_ref[used:] = jnp.zeros_like(tiles_ref[used:])


def turn(dec_ref, owner_ref, offset_ref, got_ref, o_ref):
    side = o_ref.shape[0] // MOST
    row = dec_ref[0] // side
    o_ref[...] = jnp.zeros_like(o_ref)
    for p in range(got_ref.shape[0]):
        owner = owner_ref[p]

        @pl.when(owner // side == row)
        def _(p=p, owner=owner):
            o_ref[owner % side * MOST + offset_ref[p] // 8] = got_ref[p]


def unpack(a_ref, lat_ref, rope_ref):
    per = a_ref.shape[2]
    toks = lat_ref.shape[0] // MOST
    across = LATENT // LANES
    down = toks // ROWS
    for m in range(MOST):
        for i in range(down):
            for j in range(across):
                lat_ref[
                    m * toks + ROWS * i : m * toks + ROWS * (i + 1), LANES * j : LANES * (j + 1)
                ] = a_ref[(i * across + j) // per, m, (i * across + j) % per]
        for i in range(ROPE // ROWS):
            t = down * across + i
            rope_ref[ROWS * i : ROWS * (i + 1), m * toks : (m + 1) * toks] = a_ref[
                t // per, m, t % per
            ]


def attend(shifts, before, seq_ref, len_ref, q_ref, p_ref, cos_ref, sin_ref, *rest):
    count = len(shifts)
    chips = q_ref.shape[0]
    lat_refs, w_refs, rest = rest[:chips], rest[chips : chips + count], rest[chips + count :]
    if before:
        old_ref, rest = rest[0], rest[1:]
    own_ref, send_ref, lat_s, k_s, v_s, q_s = rest
    if before:
        send_ref[:before] = old_ref[...]
    toks = q_ref.shape[3]
    pair = 2 * toks
    s = seq_ref[0]
    c = s % 2
    x = s // 2
    size = len_ref[0]
    scale = float(np.log2(np.e) / np.sqrt(QK))
    row = lax.broadcasted_iota(jnp.int32, (pair, 1), 0)
    pos = jnp.where(row < toks, c * toks + row, (1 - c) * toks + row - toks)
    causal = lax.broadcasted_iota(jnp.int32, (pair, pair), 1) <= pos
    alive = x * pair + pos < size
    heads = own_ref.shape[2] // VDIM
    slots = k_s.shape[0]

    def queries(n, chip, i):
        base = i * QK
        for j, (ref, block) in enumerate(((q_ref, s), (p_ref, s + 1 - 2 * c))):
            span = slice(j * toks, (j + 1) * toks)
            a = ref[chip, c, base + NOPE : base + NOPE + HALF].astype(F32)
            b = ref[chip, c, base + NOPE + HALF : base + QK].astype(F32)
            co = cos_ref[block]
            si = sin_ref[block]
            rot = [a * co - b * si, b * co + a * si, ones]
            q_s[n, span, :NOPE] = ref[chip, c, base : base + NOPE].T
            q_s[n, span, NOPE:] = jnp.concatenate(rot, axis=0).astype(BF).T

    lane = lax.broadcasted_iota(jnp.int32, (pair, 2 * ROPE), 1)
    for k in range(chips):
        rows = slice(k * pair, (k + 1) * pair)
        lat_s[rows] = lat_refs[k][:, :LATENT]
        tail = lat_refs[k][:, LATENT:]
        if k:
            bias = jnp.where(k <= x, 0.0, FAR)
            tail = jnp.where(lane == ROPE, bias, tail.astype(F32)).astype(BF)
        for n in range(slots):
            k_s[n, rows, NOPE:] = tail
    ones = (lax.broadcasted_iota(jnp.int32, (ROPE, toks), 0) == 0).astype(F32)
    for r in range(count):
        chip = lax.rem(x + shifts[r], chips)
        for i in range(heads):
            n = (r * heads + i) % slots
            cols = slice(i * (NOPE + VDIM), (i + 1) * (NOPE + VDIM))
            kv = jnp.dot(
                lat_s[...], w_refs[r][:, cols], preferred_element_type=F32
            )
            k_s[n, :, :NOPE] = kv[:, :NOPE].astype(BF)
            v_s[n] = kv[:, NOPE:].astype(BF)
            queries(n, chip, i)
            dots = lax.dot_general(
                q_s[n], k_s[n], (((1,), (1,)), ((), ())), preferred_element_type=F32
            )
            near = jnp.where(causal, dots[:, :pair], FAR)
            dots = jnp.concatenate([near, dots[:, pair:]], axis=1)
            top = jnp.max(dots, axis=1, keepdims=True)
            probs = jnp.exp2((dots - top) * scale)
            total = jnp.sum(probs, axis=1, keepdims=True)
            out = jnp.dot(probs.astype(BF), v_s[n], preferred_element_type=F32)
            out = jnp.where(alive, out / total, 0.0).astype(BF)
            own_ref[r, :, i * VDIM : (i + 1) * VDIM] = out[:toks]
            send_ref[before + r, :, i * VDIM : (i + 1) * VDIM] = out[toks:]


def lay_out(shifts, seq_ref, near_ref, far_ref, back_ref, o_ref):
    chips, _, width = back_ref.shape
    near = near_ref.shape[0]
    s = seq_ref[0]
    c = s % 2
    for r, shift in enumerate(shifts):
        base = lax.rem(s // 2 + shift, chips) * 2 * width
        mine = pl.multiple_of(base + c * width, width)
        other = pl.multiple_of(base + (1 - c) * width, width)
        o_ref[:, pl.ds(mine, width)] = near_ref[r] if r < near else far_ref[r - near]
        o_ref[:, pl.ds(other, width)] = back_ref[r]


def cost(flops, moved, exps=0):
    return pl.CostEstimate(flops=flops, bytes_accessed=moved, transcendentals=exps)


def shards(queries, kv_latent, key_rope, kv_gain, w_kv_up, prefix_len, page_owner, page_offset):
    toks = queries.shape[1]
    heads = queries.shape[2]
    n_seq = lax.axis_size("seq")
    n_dec = lax.axis_size("dec")
    chips = n_seq // 2
    length = toks * n_seq
    per = heads // n_seq
    cos, sin = rotation(length, toks)
    seq = jnp.reshape(lax.axis_index("seq"), (1,)).astype(jnp.int32)
    dec = jnp.reshape(lax.axis_index("dec"), (1,)).astype(jnp.int32)

    def along_x(a, k):
        return lax.ppermute(a, "seq", [(i, (i + 2 * k) % n_seq) for i in range(n_seq)])

    def partner(a):
        return lax.ppermute(a, "seq", [(i, i ^ 1) for i in range(n_seq)])

    w_left, w_right = along_x(w_kv_up, 1), along_x(w_kv_up, -1)

    q = jnp.transpose(queries[0], (1, 2, 0)).reshape(chips, 2, per * QK, toks)
    q_partner = partner(q)
    q_partner, kv_latent = lax.optimization_barrier((q_partner, kv_latent))

    side = 8
    used = toks * (LATENT + ROPE) // (ROWS * LANES)
    few = -(-used // side)
    wide, tiles = pl.pallas_call(
        prepare,
        in_specs=[SMEM, SMEM] + [VMEM] * 5,
        out_specs=[VMEM, VMEM],
        out_shape=[
            jax.ShapeDtypeStruct((toks, WIDE), BF),
            jax.ShapeDtypeStruct((side * few, ROWS, LANES), BF),
        ],
        cost_estimate=cost(500000, 800000),
        name="prepare",
    )(seq, prefix_len, kv_latent[0], key_rope[0].T, kv_gain, cos, sin)

    pairs = [[2 * i, 2 * i + 1] for i in range(chips)]
    chip_wide = lax.all_gather(wide, "seq", axis=0, axis_index_groups=pairs, tiled=True)
    all_wide = [chip_wide] + [along_x(chip_wide, k) for k in range(1, chips)]
    w_later, all_wide[1] = lax.optimization_barrier((w_kv_up, all_wide[1]))
    w_far = along_x(w_later, 2)

    rows = [[i * side + j for j in range(side)] for i in range(side)]
    columns = [[i * side + j for i in range(side)] for j in range(side)]

    def exchange(a, groups):
        return lax.all_to_all(a, "dec", 0, 0, axis_index_groups=groups, tiled=True)

    got = exchange(tiles.reshape(side, few, ROWS, LANES), rows)
    got = exchange(jnp.broadcast_to(got[None], (side,) + got.shape), columns)

    shifts = (0, chips - 1, 1, 2)
    near = chips - 1
    weights = (w_kv_up, w_left, w_right, w_far)
    own, more = [], ()
    for first, last in ((0, near), (near, chips)):
        n = last - first
        heads_of = jax.ShapeDtypeStruct((n, toks, per * VDIM), BF)
        a, b = pl.pallas_call(
            functools.partial(attend, shifts[first:last], first),
            in_specs=[SMEM, SMEM] + [VMEM] * (4 + chips + n + len(more)),
            out_specs=[VMEM, VMEM],
            out_shape=[heads_of, jax.ShapeDtypeStruct((last, toks, per * VDIM), BF)],
            scratch_shapes=[
                pltpu.VMEM((length, LATENT), BF),
                pltpu.VMEM((2, length, NOPE + 2 * ROPE), BF),
                pltpu.VMEM((2, length, VDIM), BF),
                pltpu.VMEM((2, 2 * toks, NOPE + 2 * ROPE), BF),
            ],
            compiler_params=pltpu.CompilerParams(vmem_limit_bytes=36 * 2**20),
            cost_estimate=cost(n * 2 * 10**9, n * 10**6, n * 10**6),
            name="attend",
        )(seq, prefix_len, q, q_partner, cos, sin, *all_wide, *weights[first:last], *more)
        own.append(a)
        if not more:
            got, b = lax.optimization_barrier((got, b))
            turned = pl.pallas_call(
                turn,
                in_specs=[SMEM, SMEM, SMEM, VMEM],
                out_specs=VMEM,
                out_shape=jax.ShapeDtypeStruct((side * MOST, few, ROWS, LANES), BF),
                cost_estimate=cost(0, 2000000),
                name="turn",
            )(dec, page_owner, page_offset, got.reshape(n_dec, few, ROWS, LANES))
            pool = exchange(turned.reshape(side, MOST, few, ROWS, LANES), rows)
        more = (b,)
    back = partner(b)

    attn_out = pl.pallas_call(
        functools.partial(lay_out, shifts),
        in_specs=[SMEM] + [VMEM] * 3,
        out_specs=VMEM,
        out_shape=jax.ShapeDtypeStruct((toks, heads * VDIM), BF),
        cost_estimate=cost(0, 2000000),
        name="lay_out",
    )(seq, *own, back)

    pool_lat, pool_rope = pl.pallas_call(
        unpack,
        in_specs=[VMEM],
        out_specs=[VMEM, VMEM],
        out_shape=[
            jax.ShapeDtypeStruct((MOST * toks, LATENT), BF),
            jax.ShapeDtypeStruct((ROPE, MOST * toks), BF),
        ],
        cost_estimate=cost(0, 600000),
        name="unpack",
    )(pool)
    return attn_out[None], pool_lat[None], pool_rope.T[None]


def solution(mesh):
    return jax.shard_map(
        shards,
        mesh=mesh,
        in_specs=(
            P("dec", "seq", None, None),
            P("dec", "seq", None),
            P("dec", "seq", None),
            P(),
            P(None, "seq"),
            P("dec"),
            P(),
            P(),
        ),
        out_specs=(P("dec", "seq", None), P("dec", "seq", None), P("dec", "seq", None)),
        check_vma=False,
    )
```

```python
import functools

import jax
import jax.numpy as jnp
import numpy as np
from jax import lax
from jax.experimental import pallas as pl
from jax.experimental.pallas import tpu as pltpu
from jax.sharding import PartitionSpec as P

NOPE = 128
ROPE = 64
HALF = ROPE // 2
QK = NOPE + ROPE
VDIM = 128
LATENT = 512
PAGE = 16
MOST = 2
WIDE = LATENT + 2 * ROPE
ROWS = 16
LANES = 128
FAR = -1e30
BF = jnp.bfloat16
F32 = jnp.float32
VMEM = pl.BlockSpec(memory_space=pltpu.VMEM)
SMEM = pl.BlockSpec(memory_space=pltpu.SMEM)


def rotation(length, toks):
    freq = 50000.0 ** (-2.0 * np.arange(HALF, dtype=np.float64) / ROPE)
    angle = freq[:, None] * np.arange(length, dtype=np.float64)[None, :]
    angle = angle.reshape(HALF, length // toks, toks).transpose(1, 0, 2)
    return np.cos(angle).astype(np.float32), np.sin(angle).astype(np.float32)


def prepare(seq_ref, len_ref, lat_ref, rope_ref, gain_ref, cos_ref, sin_ref, wide_ref, tiles_ref):
    toks = lat_ref.shape[0]
    x = lat_ref[...].astype(F32)
    scale = lax.rsqrt(jnp.mean(x * x, axis=-1, keepdims=True) + 1e-06)
    lat = x * scale * gain_ref[...][None, :].astype(F32)
    a = rope_ref[:HALF].astype(F32)
    b = rope_ref[HALF:].astype(F32)
    c = cos_ref[seq_ref[0]]
    s = sin_ref[seq_ref[0]]
    rot = jnp.concatenate([a * c - b * s, b * c + a * s], axis=0)
    wide_ref[:, :LATENT] = lat.astype(BF)
    padded = jnp.concatenate([rot, jnp.zeros_like(rot)], axis=0)
    wide_ref[:, LATENT:] = padded.T.astype(BF)
    kept = PAGE * ((len_ref[0] + PAGE - 1) // PAGE) - seq_ref[0] * toks
    rows = lax.broadcasted_iota(jnp.int32, lat.shape, 0)
    lat = jnp.where(rows < kept, lat, 0.0).astype(BF)
    lanes = lax.broadcasted_iota(jnp.int32, rot.shape, 1)
    rot = jnp.where(lanes < kept, rot, 0.0).astype(BF)
    across = LATENT // LANES
    down = toks // ROWS
    for i in range(down):
        for j in range(across):
            tiles_ref[i * across + j] = lat[
                ROWS * i : ROWS * (i + 1), LANES * j : LANES * (j + 1)
            ]
    for i in range(ROPE // ROWS):
        tiles_ref[down * across + i] = rot[ROWS * i : ROWS * (i + 1)]
    used = down * across + ROPE // ROWS
    tiles_ref[used:] = jnp.zeros_like(tiles_ref[used:])


def turn(owner_ref, offset_ref, got_ref, o_ref):
    o_ref[...] = jnp.zeros_like(o_ref)
    for p in range(got_ref.shape[0]):
        o_ref[owner_ref[p] * MOST + offset_ref[p] // 8] = got_ref[p]


def unpack(a_ref, lat_ref, rope_ref):
    toks = lat_ref.shape[0] // MOST
    across = LATENT // LANES
    down = toks // ROWS
    for m in range(MOST):
        for i in range(down):
            for j in range(across):
                lat_ref[
                    m * toks + ROWS * i : m * toks + ROWS * (i + 1), LANES * j : LANES * (j + 1)
                ] = a_ref[i * across + j, m]
        for i in range(ROPE // ROWS):
            rope_ref[ROWS * i : ROWS * (i + 1), m * toks : (m + 1) * toks] = a_ref[
                down * across + i, m
            ]


def attend(shifts, before, seq_ref, len_ref, q_ref, p_ref, cos_ref, sin_ref, *rest):
    count = len(shifts)
    chips = q_ref.shape[0]
    lat_refs, rest = rest[:chips], rest[chips:]
    if before:
        w_refs, old_ref, rest = rest[:2], rest[2], rest[3:]
    else:
        w_refs, rest = rest[:count], rest[count:]
    own_ref, send_ref, lat_s, k_s, v_s, q_s, w_s = rest
    depth = LATENT // 2
    if before:
        send_ref[:before] = old_ref[...]
        for j in range(2):
            w_s[j * depth : (j + 1) * depth] = w_refs[j][...]
        w_refs = [w_s]
    toks = q_ref.shape[3]
    pair = 2 * toks
    s = seq_ref[0]
    c = s % 2
    x = s // 2
    size = len_ref[0]
    scale = float(np.log2(np.e) / np.sqrt(QK))
    row = lax.broadcasted_iota(jnp.int32, (pair, 1), 0)
    pos = jnp.where(row < toks, c * toks + row, (1 - c) * toks + row - toks)
    causal = lax.broadcasted_iota(jnp.int32, (pair, pair), 1) <= pos
    alive = x * pair + pos < size
    heads = own_ref.shape[2] // VDIM
    slots = k_s.shape[0]

    def queries(n, chip, i):
        base = i * QK
        for j, (ref, block) in enumerate(((q_ref, s), (p_ref, s + 1 - 2 * c))):
            span = slice(j * toks, (j + 1) * toks)
            a = ref[chip, c, base + NOPE : base + NOPE + HALF].astype(F32)
            b = ref[chip, c, base + NOPE + HALF : base + QK].astype(F32)
            co = cos_ref[block]
            si = sin_ref[block]
            rot = [a * co - b * si, b * co + a * si, ones]
            q_s[n, span, :NOPE] = ref[chip, c, base : base + NOPE].T
            q_s[n, span, NOPE:] = jnp.concatenate(rot, axis=0).astype(BF).T

    lane = lax.broadcasted_iota(jnp.int32, (pair, 2 * ROPE), 1)
    for k in range(chips):
        rows = slice(k * pair, (k + 1) * pair)
        lat_s[rows] = lat_refs[k][:, :LATENT]
        tail = lat_refs[k][:, LATENT:]
        if k:
            bias = jnp.where(k <= x, 0.0, FAR)
            tail = jnp.where(lane == ROPE, bias, tail.astype(F32)).astype(BF)
        for n in range(slots):
            k_s[n, rows, NOPE:] = tail
    ones = (lax.broadcasted_iota(jnp.int32, (ROPE, toks), 0) == 0).astype(F32)
    for r in range(count):
        chip = lax.rem(x + shifts[r], chips)
        for i in range(heads):
            n = (r * heads + i) % slots
            cols = slice(i * (NOPE + VDIM), (i + 1) * (NOPE + VDIM))
            kv = jnp.dot(
                lat_s[...], w_refs[r][:, cols], preferred_element_type=F32
            )
            k_s[n, :, :NOPE] = kv[:, :NOPE].astype(BF)
            v_s[n] = kv[:, NOPE:].astype(BF)
            queries(n, chip, i)
            dots = lax.dot_general(
                q_s[n], k_s[n], (((1,), (1,)), ((), ())), preferred_element_type=F32
            )
            near = jnp.where(causal, dots[:, :pair], FAR)
            dots = jnp.concatenate([near, dots[:, pair:]], axis=1)
            top = jnp.max(dots, axis=1, keepdims=True)
            probs = jnp.exp2((dots - top) * scale)
            total = jnp.sum(probs, axis=1, keepdims=True)
            out = jnp.dot(probs.astype(BF), v_s[n], preferred_element_type=F32)
            out = jnp.where(alive, out / total, 0.0).astype(BF)
            own_ref[r, :, i * VDIM : (i + 1) * VDIM] = out[:toks]
            send_ref[before + r, :, i * VDIM : (i + 1) * VDIM] = out[toks:]


def lay_out(shifts, seq_ref, near_ref, far_ref, back_ref, o_ref):
    chips, _, width = back_ref.shape
    near = near_ref.shape[0]
    s = seq_ref[0]
    c = s % 2
    for r, shift in enumerate(shifts):
        base = lax.rem(s // 2 + shift, chips) * 2 * width
        mine = pl.multiple_of(base + c * width, width)
        other = pl.multiple_of(base + (1 - c) * width, width)
        o_ref[:, pl.ds(mine, width)] = near_ref[r] if r < near else far_ref[r - near]
        o_ref[:, pl.ds(other, width)] = back_ref[r]


def cost(flops, moved, exps=0):
    return pl.CostEstimate(flops=flops, bytes_accessed=moved, transcendentals=exps)


def shards(queries, kv_latent, key_rope, kv_gain, w_kv_up, prefix_len, page_owner, page_offset):
    toks = queries.shape[1]
    heads = queries.shape[2]
    n_seq = lax.axis_size("seq")
    n_dec = lax.axis_size("dec")
    chips = n_seq // 2
    length = toks * n_seq
    per = heads // n_seq
    cos, sin = rotation(length, toks)
    seq = jnp.reshape(lax.axis_index("seq"), (1,)).astype(jnp.int32)

    def along_x(a, k):
        return lax.ppermute(a, "seq", [(i, (i + 2 * k) % n_seq) for i in range(n_seq)])

    def partner(a):
        return lax.ppermute(a, "seq", [(i, i ^ 1) for i in range(n_seq)])

    w_left = along_x(w_kv_up, 1)
    w_right = along_x(w_kv_up, -1)
    depth = LATENT // 2
    w_far = (along_x(w_left[:depth], 1), along_x(w_right[depth:], -1))

    q = jnp.transpose(queries[0], (1, 2, 0)).reshape(chips, 2, per * QK, toks)
    q_partner = partner(q)
    q_partner, kv_latent = lax.optimization_barrier((q_partner, kv_latent))

    wide, tiles = pl.pallas_call(
        prepare,
        in_specs=[SMEM, SMEM] + [VMEM] * 5,
        out_specs=[VMEM, VMEM],
        out_shape=[
            jax.ShapeDtypeStruct((toks, WIDE), BF),
            jax.ShapeDtypeStruct((n_dec, ROWS, LANES), BF),
        ],
        cost_estimate=cost(500000, 800000),
        name="prepare",
    )(seq, prefix_len, kv_latent[0], key_rope[0].T, kv_gain, cos, sin)

    pairs = [[2 * i, 2 * i + 1] for i in range(chips)]
    chip_wide = lax.all_gather(wide, "seq", axis=0, axis_index_groups=pairs, tiled=True)
    all_wide = [chip_wide] + [along_x(chip_wide, k) for k in range(1, chips)]

    got = lax.all_to_all(tiles, "dec", split_axis=0, concat_axis=0, tiled=True)
    turned = pl.pallas_call(
        turn,
        in_specs=[SMEM, SMEM, VMEM],
        out_specs=VMEM,
        out_shape=jax.ShapeDtypeStruct((n_dec * MOST, ROWS, LANES), BF),
        cost_estimate=cost(0, 800000),
        name="turn",
    )(page_owner, page_offset, got)
    pool = lax.all_to_all(
        turned.reshape(n_dec, MOST, ROWS, LANES), "dec", split_axis=0, concat_axis=0, tiled=True
    )

    shifts = (0, chips - 1, 1, 2)
    near = chips - 1
    own, more = [], (w_kv_up, w_left, w_right)
    for first, last in ((0, near), (near, chips)):
        n = last - first
        heads_of = jax.ShapeDtypeStruct((n, toks, per * VDIM), BF)
        a, b = pl.pallas_call(
            functools.partial(attend, shifts[first:last], first),
            in_specs=[SMEM, SMEM] + [VMEM] * (4 + chips + len(more)),
            out_specs=[VMEM, VMEM],
            out_shape=[heads_of, jax.ShapeDtypeStruct((last, toks, per * VDIM), BF)],
            scratch_shapes=[
                pltpu.VMEM((length, LATENT), BF),
                pltpu.VMEM((2, length, NOPE + 2 * ROPE), BF),
                pltpu.VMEM((2, length, VDIM), BF),
                pltpu.VMEM((2, 2 * toks, NOPE + 2 * ROPE), BF),
                pltpu.VMEM(w_kv_up.shape, BF),
            ],
            compiler_params=pltpu.CompilerParams(vmem_limit_bytes=40 * 2**20),
            cost_estimate=cost(n * 2 * 10**9, n * 10**6, n * 10**6),
            name="attend",
        )(seq, prefix_len, q, q_partner, cos, sin, *all_wide, *more)
        own.append(a)
        more = (*w_far, b)
    back = partner(b)

    pool_lat, pool_rope = pl.pallas_call(
        unpack,
        in_specs=[VMEM],
        out_specs=[VMEM, VMEM],
        out_shape=[
            jax.ShapeDtypeStruct((MOST * toks, LATENT), BF),
            jax.ShapeDtypeStruct((ROPE, MOST * toks), BF),
        ],
        cost_estimate=cost(0, 600000),
        name="unpack",
    )(pool)
    back, pool_lat, pool_rope = lax.optimization_barrier((back, pool_lat, pool_rope))

    attn_out = pl.pallas_call(
        functools.partial(lay_out, shifts),
        in_specs=[SMEM] + [VMEM] * 3,
        out_specs=VMEM,
        out_shape=jax.ShapeDtypeStruct((toks, heads * VDIM), BF),
        cost_estimate=cost(0, 2000000),
        name="lay_out",
    )(seq, *own, back)
    return attn_out[None], pool_lat[None], pool_rope.T[None]


def solution(mesh):
    return jax.shard_map(
        shards,
        mesh=mesh,
        in_specs=(
            P("dec", "seq", None, None),
            P("dec", "seq", None),
            P("dec", "seq", None),
            P(),
            P(None, "seq"),
            P("dec"),
            P(),
            P(),
        ),
        out_specs=(P("dec", "seq", None), P("dec", "seq", None), P("dec", "seq", None)),
        check_vma=False,
    )
```

```python
import functools

import jax
import jax.numpy as jnp
import numpy as np
from jax import lax
from jax.experimental import pallas as pl
from jax.experimental.pallas import tpu as pltpu
from jax.sharding import PartitionSpec as P

NOPE = 128
ROPE = 64
HALF = ROPE // 2
QK = NOPE + ROPE
VDIM = 128
LATENT = 512
PAGE = 16
MOST = 2
WIDE = LATENT + 2 * ROPE
ROWS = 16
LANES = 128
FAR = -1e30
BF = jnp.bfloat16
F32 = jnp.float32
VMEM = pl.BlockSpec(memory_space=pltpu.VMEM)
SMEM = pl.BlockSpec(memory_space=pltpu.SMEM)


def rotation(length, toks):
    freq = 50000.0 ** (-2.0 * np.arange(HALF, dtype=np.float64) / ROPE)
    angle = freq[:, None] * np.arange(length, dtype=np.float64)[None, :]
    angle = angle.reshape(HALF, length // toks, toks).transpose(1, 0, 2)
    return np.cos(angle).astype(np.float32), np.sin(angle).astype(np.float32)


def prepare(seq_ref, len_ref, lat_ref, rope_ref, gain_ref, cos_ref, sin_ref, wide_ref, tiles_ref):
    toks = lat_ref.shape[0]
    x = lat_ref[...].astype(F32)
    scale = lax.rsqrt(jnp.mean(x * x, axis=-1, keepdims=True) + 1e-06)
    lat = x * scale * gain_ref[...][None, :].astype(F32)
    a = rope_ref[:HALF].astype(F32)
    b = rope_ref[HALF:].astype(F32)
    c = cos_ref[seq_ref[0]]
    s = sin_ref[seq_ref[0]]
    rot = jnp.concatenate([a * c - b * s, b * c + a * s], axis=0)
    wide_ref[:, :LATENT] = lat.astype(BF)
    padded = jnp.concatenate([rot, jnp.zeros_like(rot)], axis=0)
    wide_ref[:, LATENT:] = padded.T.astype(BF)
    kept = PAGE * ((len_ref[0] + PAGE - 1) // PAGE) - seq_ref[0] * toks
    rows = lax.broadcasted_iota(jnp.int32, lat.shape, 0)
    lat = jnp.where(rows < kept, lat, 0.0).astype(BF)
    lanes = lax.broadcasted_iota(jnp.int32, rot.shape, 1)
    rot = jnp.where(lanes < kept, rot, 0.0).astype(BF)
    across = LATENT // LANES
    down = toks // ROWS
    for i in range(down):
        for j in range(across):
            tiles_ref[i * across + j] = lat[
                ROWS * i : ROWS * (i + 1), LANES * j : LANES * (j + 1)
            ]
    for i in range(ROPE // ROWS):
        tiles_ref[down * across + i] = rot[ROWS * i : ROWS * (i + 1)]
    used = down * across + ROPE // ROWS
    tiles_ref[used:] = jnp.zeros_like(tiles_ref[used:])


def turn(owner_ref, offset_ref, got_ref, o_ref):
    o_ref[...] = jnp.zeros_like(o_ref)
    for p in range(got_ref.shape[0]):
        o_ref[owner_ref[p] * MOST + offset_ref[p] // 8] = got_ref[p]


def unpack(a_ref, lat_ref, rope_ref):
    toks = lat_ref.shape[0] // MOST
    across = LATENT // LANES
    down = toks // ROWS
    for m in range(MOST):
        for i in range(down):
            for j in range(across):
                lat_ref[
                    m * toks + ROWS * i : m * toks + ROWS * (i + 1), LANES * j : LANES * (j + 1)
                ] = a_ref[i * across + j, m]
        for i in range(ROPE // ROWS):
            rope_ref[ROWS * i : ROWS * (i + 1), m * toks : (m + 1) * toks] = a_ref[
                down * across + i, m
            ]


def attend(shifts, before, seq_ref, len_ref, q_ref, p_ref, cos_ref, sin_ref, *rest):
    count = len(shifts)
    chips = q_ref.shape[0]
    lat_refs, rest = rest[:chips], rest[chips:]
    w_refs, rest = rest[:count], rest[count:]
    if before:
        old_ref, rest = rest[0], rest[1:]
    own_ref, send_ref, lat_s, k_s, v_s, q_s = rest
    if before:
        send_ref[:before] = old_ref[...]
    toks = q_ref.shape[3]
    pair = 2 * toks
    s = seq_ref[0]
    c = s % 2
    x = s // 2
    size = len_ref[0]
    scale = float(np.log2(np.e) / np.sqrt(QK))
    row = lax.broadcasted_iota(jnp.int32, (pair, 1), 0)
    pos = jnp.where(row < toks, c * toks + row, (1 - c) * toks + row - toks)
    causal = lax.broadcasted_iota(jnp.int32, (pair, pair), 1) <= pos
    alive = x * pair + pos < size
    heads = own_ref.shape[2] // VDIM
    slots = k_s.shape[0]

    def queries(n, chip, i):
        base = i * QK
        for j, (ref, block) in enumerate(((q_ref, s), (p_ref, s + 1 - 2 * c))):
            span = slice(j * toks, (j + 1) * toks)
            a = ref[chip, c, base + NOPE : base + NOPE + HALF].astype(F32)
            b = ref[chip, c, base + NOPE + HALF : base + QK].astype(F32)
            co = cos_ref[block]
            si = sin_ref[block]
            rot = [a * co - b * si, b * co + a * si, ones]
            q_s[n, span, :NOPE] = ref[chip, c, base : base + NOPE].T
            q_s[n, span, NOPE:] = jnp.concatenate(rot, axis=0).astype(BF).T

    lane = lax.broadcasted_iota(jnp.int32, (pair, 2 * ROPE), 1)
    for k in range(chips):
        rows = slice(k * pair, (k + 1) * pair)
        lat_s[rows] = lat_refs[k][:, :LATENT]
        tail = lat_refs[k][:, LATENT:]
        if k:
            bias = jnp.where(k <= x, 0.0, FAR)
            tail = jnp.where(lane == ROPE, bias, tail.astype(F32)).astype(BF)
        for n in range(slots):
            k_s[n, rows, NOPE:] = tail
    ones = (lax.broadcasted_iota(jnp.int32, (ROPE, toks), 0) == 0).astype(F32)
    for r in range(count):
        chip = lax.rem(x + shifts[r], chips)
        for i in range(heads):
            n = (r * heads + i) % slots
            cols = slice(i * (NOPE + VDIM), (i + 1) * (NOPE + VDIM))
            kv = jnp.dot(
                lat_s[...], w_refs[r][:, cols], preferred_element_type=F32
            )
            k_s[n, :, :NOPE] = kv[:, :NOPE].astype(BF)
            v_s[n] = kv[:, NOPE:].astype(BF)
            queries(n, chip, i)
            dots = lax.dot_general(
                q_s[n], k_s[n], (((1,), (1,)), ((), ())), preferred_element_type=F32
            )
            near = jnp.where(causal, dots[:, :pair], FAR)
            dots = jnp.concatenate([near, dots[:, pair:]], axis=1)
            top = jnp.max(dots, axis=1, keepdims=True)
            probs = jnp.exp2((dots - top) * scale)
            total = jnp.sum(probs, axis=1, keepdims=True)
            out = jnp.dot(probs.astype(BF), v_s[n], preferred_element_type=F32)
            out = jnp.where(alive, out / total, 0.0).astype(BF)
            own_ref[r, :, i * VDIM : (i + 1) * VDIM] = out[:toks]
            send_ref[before + r, :, i * VDIM : (i + 1) * VDIM] = out[toks:]


def lay_out(shifts, seq_ref, near_ref, far_ref, back_ref, o_ref):
    chips, _, width = back_ref.shape
    near = near_ref.shape[0]
    s = seq_ref[0]
    c = s % 2
    for r, shift in enumerate(shifts):
        base = lax.rem(s // 2 + shift, chips) * 2 * width
        mine = pl.multiple_of(base + c * width, width)
        other = pl.multiple_of(base + (1 - c) * width, width)
        o_ref[:, pl.ds(mine, width)] = near_ref[r] if r < near else far_ref[r - near]
        o_ref[:, pl.ds(other, width)] = back_ref[r]


def cost(flops, moved, exps=0):
    return pl.CostEstimate(flops=flops, bytes_accessed=moved, transcendentals=exps)


def shards(queries, kv_latent, key_rope, kv_gain, w_kv_up, prefix_len, page_owner, page_offset):
    toks = queries.shape[1]
    heads = queries.shape[2]
    n_seq = lax.axis_size("seq")
    n_dec = lax.axis_size("dec")
    chips = n_seq // 2
    length = toks * n_seq
    per = heads // n_seq
    cos, sin = rotation(length, toks)
    seq = jnp.reshape(lax.axis_index("seq"), (1,)).astype(jnp.int32)

    def along_x(a, k):
        return lax.ppermute(a, "seq", [(i, (i + 2 * k) % n_seq) for i in range(n_seq)])

    def partner(a):
        return lax.ppermute(a, "seq", [(i, i ^ 1) for i in range(n_seq)])

    w_left = along_x(w_kv_up, 1)
    w_right = along_x(w_kv_up, -1)
    q = jnp.transpose(queries[0], (1, 2, 0)).reshape(chips, 2, per * QK, toks)
    q_partner = partner(q)
    q_partner, kv_latent = lax.optimization_barrier((q_partner, kv_latent))

    wide, tiles = pl.pallas_call(
        prepare,
        in_specs=[SMEM, SMEM] + [VMEM] * 5,
        out_specs=[VMEM, VMEM],
        out_shape=[
            jax.ShapeDtypeStruct((toks, WIDE), BF),
            jax.ShapeDtypeStruct((n_dec, ROWS, LANES), BF),
        ],
        cost_estimate=cost(500000, 800000),
        name="prepare",
    )(seq, prefix_len, kv_latent[0], key_rope[0].T, kv_gain, cos, sin)

    pairs = [[2 * i, 2 * i + 1] for i in range(chips)]
    chip_wide = lax.all_gather(wide, "seq", axis=0, axis_index_groups=pairs, tiled=True)
    all_wide = [chip_wide] + [along_x(chip_wide, k) for k in range(1, chips)]
    w_far = along_x(lax.optimization_barrier((w_left, chip_wide))[0], 1)

    got = lax.all_to_all(tiles, "dec", split_axis=0, concat_axis=0, tiled=True)
    turned = pl.pallas_call(
        turn,
        in_specs=[SMEM, SMEM, VMEM],
        out_specs=VMEM,
        out_shape=jax.ShapeDtypeStruct((n_dec * MOST, ROWS, LANES), BF),
        cost_estimate=cost(0, 800000),
        name="turn",
    )(page_owner, page_offset, got)
    pool = lax.all_to_all(
        turned.reshape(n_dec, MOST, ROWS, LANES), "dec", split_axis=0, concat_axis=0, tiled=True
    )

    shifts = (0, chips - 1, 1, 2)
    near = chips - 1
    own, more = [], (w_kv_up, w_left, w_right)
    for first, last in ((0, near), (near, chips)):
        n = last - first
        heads_of = jax.ShapeDtypeStruct((n, toks, per * VDIM), BF)
        a, b = pl.pallas_call(
            functools.partial(attend, shifts[first:last], first),
            in_specs=[SMEM, SMEM] + [VMEM] * (4 + chips + len(more)),
            out_specs=[VMEM, VMEM],
            out_shape=[heads_of, jax.ShapeDtypeStruct((last, toks, per * VDIM), BF)],
            scratch_shapes=[
                pltpu.VMEM((length, LATENT), BF),
                pltpu.VMEM((2, length, NOPE + 2 * ROPE), BF),
                pltpu.VMEM((2, length, VDIM), BF),
                pltpu.VMEM((2, 2 * toks, NOPE + 2 * ROPE), BF),
            ],
            compiler_params=pltpu.CompilerParams(vmem_limit_bytes=40 * 2**20),
            cost_estimate=cost(n * 2 * 10**9, n * 10**6, n * 10**6),
            name="attend",
        )(seq, prefix_len, q, q_partner, cos, sin, *all_wide, *more)
        own.append(a)
        more = (w_far, b)
    back = partner(b)

    pool_lat, pool_rope = pl.pallas_call(
        unpack,
        in_specs=[VMEM],
        out_specs=[VMEM, VMEM],
        out_shape=[
            jax.ShapeDtypeStruct((MOST * toks, LATENT), BF),
            jax.ShapeDtypeStruct((ROPE, MOST * toks), BF),
        ],
        cost_estimate=cost(0, 600000),
        name="unpack",
    )(pool)
    back, pool_lat, pool_rope = lax.optimization_barrier((back, pool_lat, pool_rope))

    attn_out = pl.pallas_call(
        functools.partial(lay_out, shifts),
        in_specs=[SMEM] + [VMEM] * 3,
        out_specs=VMEM,
        out_shape=jax.ShapeDtypeStruct((toks, heads * VDIM), BF),
        cost_estimate=cost(0, 2000000),
        name="lay_out",
    )(seq, *own, back)
    return attn_out[None], pool_lat[None], pool_rope.T[None]


def solution(mesh):
    return jax.shard_map(
        shards,
        mesh=mesh,
        in_specs=(
            P("dec", "seq", None, None),
            P("dec", "seq", None),
            P("dec", "seq", None),
            P(),
            P(None, "seq"),
            P("dec"),
            P(),
            P(),
        ),
        out_specs=(P("dec", "seq", None), P("dec", "seq", None), P("dec", "seq", None)),
        check_vma=False,
    )
```
